32 devices in a mesh: rep: 8 (over z, core), exp: 4 (over y, x).
Axes of the slice: x: 2, y: 2, z: 4, core: 2. Of those that a mesh axis runs over, the one named last changes fastest.
Arguments:
- tokens: bfloat16 [4096, 4096], P(('rep', 'exp')), may hold values from -6 to 6
- grad_out: bfloat16 [4096, 4096], P(('rep', 'exp')), may hold values from -6 to 6
- gates: float32 [4096, 2], P(('rep', 'exp')), may hold values from 0.1 to 0.9
- expert_ids: int32 [4096, 2], P(('rep', 'exp')), may hold values from 0 to 3, all different within a row; in each aligned block of 128 rows (0 to 127, 128 to 255, ...) at most 80 rows name the same one
- w_all: bfloat16 [4, 4096, 384], P('exp', 'rep'), may hold values from -0.09375 to 0.09375
- touched: int32 [8, 4, 32], P('rep', 'exp'), may hold values 0 or 1
Outputs:
- token_grad: bfloat16 [4096, 4096], P(('rep', 'exp'))
- weight_grad: float32 [4, 4096, 384], P('exp', 'rep')
The draws below stay inside these ranges and needn't reach their ends.
Inputs may be any that keep to these rules, and one draw needn't show every extreme that they name: `expert_ids`: each token names two different experts. Among the tokens of one device no expert is named more than 80 times, a bound that some block reaches.
All inputs are finite; a program needn't handle non-finite values. No bound on the sum of `touched` on one device may be relied on, other than what follows from the above.
Results may differ from the reference program's by a relative error of at most 0.017.
Values may be sent and summed in bfloat16 or wider, within the bound.
A program may use at most 64 MiB of HBM per device.

```python
import math
import jax
import jax.numpy as jnp
import numpy as np
from jax import lax

D = 4096
HID = 128
TOK_DEV = 128
EXPERTS = 4
CAP = 80
NB = 32
TOKENS = 4096
N_REP = 8
N_EXP = 4


def with_ends(array, stream_key, smallest, top_value):
    place = [jax.random.randint(jax.random.fold_in(stream_key, axis), (), 0, length) for axis, length in enumerate(array.shape)]
    widest = array.shape.index(max(array.shape))
    neighbour = place[:widest] + [(place[widest] + 1) % array.shape[widest]] + place[widest + 1:]
    return array.at[tuple(place)].set(smallest).at[tuple(neighbour)].set(top_value)


def shard_levels(key, extent, shards, smallest, high):
    def one(dim, blocks):
        steps = jax.random.uniform(jax.random.fold_in(jax.random.fold_in(key, 6), dim), (blocks,), jnp.float32, smallest / len(shards), high / len(shards))
        return jnp.repeat(jnp.exp(steps), extent[dim] // blocks).reshape((-1,) + (1,) * (len(extent) - dim - 1))

    level = one(*shards[0])
    for cut in shards[1:]:
        level = level * one(*cut)
    return level


def routed_block(own_key, own, number, rows, count, top, limit, lean):
    sequence = jax.random.permutation(own_key, count)
    crowded, ordinary = portions_of(count, rows * top, limit, lean, True), portions_of(count, rows * top, limit, lean, False)
    places = jnp.arange(count)

    def named(sizes, turn):
        used = int((sizes > 0).sum())
        fixed = max(1, used // 4)
        passed = fixed + (places - fixed + turn * (used - fixed)) % max(1, count - fixed)
        return jnp.zeros((count,), jnp.int32).at[sequence[jnp.where(places < fixed, places, passed)]].set(jnp.asarray(sizes, jnp.int32))

    sizes = jnp.where(number % 4 == 0, named(crowded, number // 4), named(ordinary, number - number // 4 - 1))
    mixed = jax.random.permutation(jax.random.fold_in(own, 3), count)
    giver, taker = mixed[0:count // 2 * 2:2], mixed[1:count // 2 * 2:2]
    margin = jnp.minimum(sizes[giver] - 1, limit - sizes[taker]) // 2
    margin = jnp.where((giver == sequence[0]) | (taker == sequence[0]) | (sizes[taker] == 0), 0, jnp.maximum(margin, 0))
    passed = jax.random.randint(jax.random.fold_in(own, 4), (count // 2,), 0, 1 << 20) % (margin + 1)
    sizes = sizes.at[giver].add(-passed).at[taker].add(passed)
    items = jnp.searchsorted(jnp.cumsum(sizes), jnp.arange(rows * top), side="right").astype(jnp.int32)
    listing = items.reshape(top, rows).T
    listing = listing[jax.random.permutation(jax.random.fold_in(own, 1), rows)]
    turn = jax.random.randint(jax.random.fold_in(own, 2), (rows, 1), 0, top)
    return jnp.take_along_axis(listing, (jnp.arange(top)[None, :] + turn) % top, axis=1)


def portions_of(amount, total, reach, lean, full):
    weights = [(1 << 20) // math.isqrt(rank ** lean) + 1 for rank in range(1, amount + 1)]
    largest = reach if full else min(reach, max(-(-total // amount), total * weights[0] // sum(weights)))
    least = 1 if total - largest >= amount - 1 else 0
    counts, rest = [largest] + [least] * (amount - 1), total - largest - least * (amount - 1)
    while rest > 0:
        candidates = [i for i in range(1, amount) if counts[i] < largest] or [i for i in range(1, amount) if counts[i] < reach]
        whole, remaining = sum([weights[i] for i in candidates]), rest
        for i in candidates:
            more = min(reach - counts[i], max(1, remaining * weights[i] // whole), rest)
            counts[i] = counts[i] + more
            rest = rest - more
    return np.array(counts)


def bell_draw(key, shape, width, bound, pieces=(), kind=jnp.bfloat16):
    loudness = shard_levels(key, shape, pieces, -0.22, 0.18) if pieces else 1.0
    entries = jax.random.normal(key, shape, jnp.float32) * width * loudness
    return jnp.minimum(jnp.maximum(entries, -bound), bound).astype(kind)


def setup_inputs(seed: int = 0) -> dict:
    key_list = jax.random.split(jax.random.key(seed), 7)
    tokens = bell_draw(key_list[0], (TOKENS, D), 1.0, 6.0, ((0, 32),))
    grad_out = bell_draw(key_list[1], (TOKENS, D), 1.0, 6.0, ((0, 32),))
    gates = jnp.clip(0.1 + 0.79999997 * jax.random.uniform(key_list[2], (TOKENS, 2), jnp.float32) ** shard_levels(key_list[2], (TOKENS, 2), ((0, 32),), -0.2, 0.2), 0.1, 0.9)
    expert_ids_keys = jax.random.split(jax.random.fold_in(key_list[3], 1), TOKENS // TOK_DEV)
    expert_ids_turns = jax.random.permutation(jax.random.fold_in(key_list[3], 3), TOKENS // TOK_DEV)
    expert_ids = jax.vmap(lambda own, number: routed_block(jax.random.fold_in(key_list[3], 2), own, number, TOK_DEV, EXPERTS, 2, CAP, 1))(expert_ids_keys, expert_ids_turns).reshape((TOKENS, 2))
    w_all = bell_draw(key_list[4], (EXPERTS, D, 3 * HID), D ** -0.5, 0.09375, ((0, 4), (1, 8)))
    touched = with_ends((jax.random.randint(key_list[5], (N_REP, EXPERTS, NB), 0, 2) < 1).astype(jnp.int32), jax.random.fold_in(key_list[5], 1), 0, 1)
    return {"tokens": tokens, "grad_out": grad_out, "gates": gates, "expert_ids": expert_ids, "w_all": w_all, "touched": touched}


def silu_terms(gate_pre):
    sigmoid_g = jax.nn.sigmoid(gate_pre)
    return gate_pre * sigmoid_g, sigmoid_g * (1.0 + gate_pre * (1.0 - sigmoid_g))


def expert_backward(slot_x, slot_dy, weights):
    hidden_count = weights.shape[1] // 3
    gate_up = jnp.dot(slot_x, weights[:, :2 * hidden_count], preferred_element_type=jnp.float32)
    hid_grad = jnp.dot(slot_dy, weights[:, 2 * hidden_count:], preferred_element_type=jnp.float32)
    gate_pre = gate_up[:, :hidden_count]
    up_pre = gate_up[:, hidden_count:]
    silu_val, silu_slope = silu_terms(gate_pre)
    hidden = (silu_val * up_pre).astype(jnp.bfloat16)
    gate_grad = (hid_grad * up_pre * silu_slope).astype(jnp.bfloat16)
    up_grad = (hid_grad * silu_val).astype(jnp.bfloat16)
    both_grad = jnp.concatenate([gate_grad, up_grad], 1)
    proj_grad = lax.dot_general(slot_x, both_grad, (((0,), (0,)), ((), ())), preferred_element_type=jnp.float32)
    down_grad = lax.dot_general(slot_dy, hidden, (((0,), (0,)), ((), ())), preferred_element_type=jnp.float32)
    full_grad = jnp.concatenate([proj_grad, down_grad], 1)
    slot_dx = lax.dot_general(both_grad, weights[:, :2 * hidden_count], (((1,), (1,)), ((), ())), preferred_element_type=jnp.float32)
    return full_grad, slot_dx.astype(jnp.bfloat16)


def reference(tokens, grad_out, gates, expert_ids, w_all, touched):
    capacity = 5 * TOK_DEV // (2 * EXPERTS)
    group_tokens = N_EXP * TOK_DEV
    slot_total = N_EXP * capacity

    def one_replica(grad_sum, replica):
        first = replica * group_tokens
        x_rep = lax.dynamic_slice_in_dim(tokens, first, group_tokens, 0)
        dy_rep = lax.dynamic_slice_in_dim(grad_out, first, group_tokens, 0)
        gate_rep = lax.dynamic_slice_in_dim(gates, first, group_tokens, 0)
        id_rep = lax.dynamic_slice_in_dim(expert_ids, first, group_tokens, 0)
        flat_ids = id_rep.reshape(N_EXP, 2 * TOK_DEV)
        onehot = (flat_ids[:, :, None] == jnp.arange(EXPERTS, dtype=jnp.int32)[None, None, :]).astype(jnp.int32)
        slot_rank = jnp.sum(jnp.cumsum(onehot, 1) * onehot, 2) - 1
        source = jnp.arange(N_EXP, dtype=jnp.int32)[:, None]
        slot_index = (flat_ids * slot_total + source * capacity + slot_rank).astype(jnp.int32)
        pair_index = jnp.arange(2 * group_tokens, dtype=jnp.int32)
        pair_table = jnp.full((EXPERTS * slot_total,), 2 * group_tokens, jnp.int32)
        pair_table = pair_table.at[slot_index.reshape(-1)].set(pair_index)
        token_table = (pair_table // 2).astype(jnp.int32)
        x_aug = jnp.concatenate([x_rep, jnp.zeros((1, D), jnp.bfloat16)], 0)
        scaled = (dy_rep.astype(jnp.float32)[:, None, :] * gate_rep[:, :, None]).astype(jnp.bfloat16)
        dy_aug = jnp.concatenate([scaled.reshape(2 * group_tokens, D), jnp.zeros((1, D), jnp.bfloat16)], 0)

        def one_expert(expert):
            pair_rows = lax.dynamic_slice_in_dim(pair_table, expert * slot_total, slot_total, 0)
            slot_x = x_aug[pair_rows // 2]
            slot_dy = dy_aug[pair_rows]
            full_grad, slot_dx = expert_backward(slot_x, slot_dy, w_all[expert])
            row_mask = jnp.repeat(touched[replica, expert].astype(jnp.float32), 128)[:, None]
            masked = lax.optimization_barrier((full_grad * row_mask).astype(jnp.bfloat16))
            return masked.astype(jnp.float32), slot_dx

        grads, slot_dxs = lax.map(one_expert, jnp.arange(EXPERTS, dtype=jnp.int32))
        token_sum = jnp.zeros((group_tokens + 1, D), jnp.float32)
        token_sum = token_sum.at[token_table].add(slot_dxs.reshape(-1, D).astype(jnp.float32))
        return grad_sum + grads, token_sum[:group_tokens].astype(jnp.bfloat16)

    start_sum = jnp.zeros((EXPERTS, D, 3 * HID), jnp.float32)
    grad_sum, token_grads = lax.scan(one_replica, start_sum, jnp.arange(N_REP, dtype=jnp.int32))
    return token_grads.reshape(N_REP * group_tokens, D), grad_sum
```

```python
import functools
import jax
import jax.numpy as jnp
from jax import lax
from jax.experimental import pallas as pl
from jax.experimental.pallas import tpu as pltpu
from jax.sharding import PartitionSpec as P

MESH = pl.DeviceIdType.MESH
BF16 = jnp.bfloat16
F32 = jnp.float32


def silu_terms(gate_pre):
    sigmoid_g = jax.nn.sigmoid(gate_pre)
    return (gate_pre * sigmoid_g, sigmoid_g * (1.0 + gate_pre * (1.0 - sigmoid_g)))


def contract_rows(left, right):
    return lax.dot_general(
        left, right, (((0,), (0,)), ((), ())), preferred_element_type=jnp.float32
    )


def kernel(
    R, E, T, S, H,
    x_ref, g_ref, w_ref, id_ref, tm_ref, gate_ref,
    dx_out, dw_out,
    X, Y, IDS, TM, W, ACC, PS, PR, AA, GU, HD, DX, DW, SB, UP, DN, FS, FW,
    a2s, a2r, wr, ws, bs, br, us, ur, loc,
):
    H2, H3 = 2 * H, 3 * H
    Z = R // 2
    r = lax.axis_index("rep")
    q = lax.axis_index("exp")
    z, c = r // 2, lax.rem(r, 2)
    sib = (2 * z + 1 - c, q)
    above = (lax.rem(r + 2, R), q)
    below = (lax.rem(r + R - 2, R), q)
    has_up, has_dn = z < Z - 1, z > 0

    barrier = pltpu.get_barrier_semaphore()
    for j in range(1, E):
        pl.semaphore_signal(barrier, inc=1, device_id=(r, lax.rem(q + j, E)), device_id_type=MESH)
    pl.semaphore_signal(barrier, inc=1, device_id=sib, device_id_type=MESH)

    @pl.when(has_up)
    def _():
        pl.semaphore_signal(barrier, inc=1, device_id=above, device_id_type=MESH)

    @pl.when(has_dn)
    def _():
        pl.semaphore_signal(barrier, inc=1, device_id=below, device_id_type=MESH)

    edge = jnp.where(z == 0, 1, 0) + jnp.where(z == Z - 1, 1, 0)
    pl.semaphore_wait(barrier, E + 2 - edge)

    def rcopy(src, dst, ss, rs, dev):
        return pltpu.make_async_remote_copy(
            src_ref=src, dst_ref=dst, send_sem=ss, recv_sem=rs, device_id=dev, device_id_type=MESH
        )

    def peer(j):
        return lax.rem(q + j, E)

    def put(kind, j, src, dst):
        return rcopy(src, dst, a2s.at[kind, j], a2r.at[kind, q], (r, peer(j)))

    def got(kind, j, dst):
        p = peer(j)
        rcopy(dst.at[p], dst.at[p], a2s.at[kind, j], a2r.at[kind, p], (r, p)).wait_recv()

    sent = []

    def start(kind, j, src, dst):
        d = put(kind, j, src, dst)
        d.start()
        sent.append(d)

    WR = W.at[r]
    for j in range(1, E):
        start(0, j, w_ref.at[peer(j)], WR.at[q])
    for j in range(1, E):
        start(1, j, id_ref, IDS.at[q])
        start(2, j, tm_ref.at[peer(j)], TM.at[q])
    for j in range(1, E):
        start(3, j, x_ref.at[peer(j)], X.at[q])
    for j in range(1, E):
        start(4, j, g_ref.at[peer(j)], Y.at[q])
    WR[q] = w_ref[q]
    IDS[q] = id_ref[...]
    TM[q] = tm_ref[q]
    X[q] = x_ref[q]
    Y[q] = g_ref[q]
    ACC[...] = jnp.zeros_like(ACC)
    for j in range(1, E):
        got(0, j, WR)

    def w_up(zz):
        s = 2 * zz + c
        return rcopy(W.at[s], W.at[s], ws.at[0, zz], wr.at[s], above)

    def w_dn(zz):
        s = 2 * zz + c
        return rcopy(W.at[s], W.at[s], ws.at[1, zz], wr.at[s], below)

    def w_sib(zz):
        s = 2 * zz + c
        return rcopy(W.at[s], W.at[s], ws.at[2, zz], wr.at[s], sib)

    def w_wait(s):
        rcopy(W.at[s], W.at[s], ws.at[0, 0], wr.at[s], sib).wait_recv()

    def project(s):
        xs = X[:, s].reshape(E * T, S)
        ys = Y[:, s].reshape(E * T, S)
        for e in range(E):
            ACC[:, e * H3 : e * H3 + H2] += jnp.dot(
                xs, W[s, e, :, :H2], preferred_element_type=F32
            )
            ACC[:, e * H3 + H2 : (e + 1) * H3] += jnp.dot(
                ys, W[s, e, :, H2:], preferred_element_type=F32
            )

    @pl.when(has_up)
    def _():
        w_up(z).start()

    @pl.when(has_dn)
    def _():
        w_dn(z).start()

    w_sib(z).start()
    for j in range(1, E):
        got(1, j, IDS)
        got(2, j, TM)
    for j in range(1, E):
        got(3, j, X)
    for j in range(1, E):
        got(4, j, Y)
    project(r)
    w_wait(2 * z + 1 - c)
    project(2 * z + 1 - c)
    for d in range(1, Z):
        lo, hi = z - d, z + d
        has_lo, has_hi = lo >= 0, hi < Z

        @pl.when(has_lo)
        def _():
            w_wait(2 * lo + c)

            @pl.when(has_up)
            def _():
                w_up(lo).start()

            w_sib(lo).start()

        @pl.when(has_hi)
        def _():
            w_wait(2 * hi + c)

            @pl.when(has_dn)
            def _():
                w_dn(hi).start()

            w_sib(hi).start()

        @pl.when(has_lo)
        def _():
            project(2 * lo + c)
            w_wait(2 * lo + 1 - c)
            project(2 * lo + 1 - c)

        @pl.when(has_hi)
        def _():
            project(2 * hi + c)
            w_wait(2 * hi + 1 - c)
            project(2 * hi + 1 - c)

    for j in list(range(1, E)) + [0]:
        p = peer(j)
        ids = IDS[p].astype(F32)
        rows = pl.ds(pl.multiple_of(p * T, T), T)
        for k in range(2):
            tot = jnp.zeros((T, H3), F32)
            for e in range(E):
                m = (ids[:, k : k + 1] == e).astype(F32)
                tot = tot + m * ACC[rows, e * H3 : (e + 1) * H3]
            PS[p, :, k * H3 : (k + 1) * H3] = tot.astype(BF16)
        if j:
            start(5, j, PS.at[p], PR.at[q])
    for j in range(1, E):
        got(5, j, PR)
    for k in range(2):
        tot = PS[q, :, k * H3 : (k + 1) * H3].astype(F32)
        for j in range(1, E):
            tot = tot + PR[peer(j), :, k * H3 : (k + 1) * H3].astype(F32)
        gate = gate_ref[:, k : k + 1]
        silu_val, silu_slope = silu_terms(tot[:, :H])
        up_pre, hid_grad = tot[:, H:H2], gate * tot[:, H2:]
        AA[q, :, k * H3 : k * H3 + H] = (hid_grad * up_pre * silu_slope).astype(BF16)
        AA[q, :, k * H3 + H : k * H3 + H2] = (hid_grad * silu_val).astype(BF16)
        AA[q, :, k * H3 + H2 : (k + 1) * H3] = (gate * (silu_val * up_pre)).astype(BF16)
    for j in range(1, E):
        start(6, j, AA.at[q], AA.at[q])
    for j in range(E):
        if j:
            got(6, j, AA)
        p = peer(j)
        ids = IDS[p].astype(F32)
        rows = pl.ds(pl.multiple_of(p * T, T), T)
        a0 = AA[p, :, :H3].astype(F32)
        a1 = AA[p, :, H3:].astype(F32)
        for e in range(E):
            m0 = (ids[:, 0:1] == e).astype(F32)
            m1 = (ids[:, 1:2] == e).astype(F32)
            v = (m0 * a0 + m1 * a1).astype(BF16)
            GU[rows, e * H2 : (e + 1) * H2] = v[:, :H2]
            HD[rows, e * H : (e + 1) * H] = v[:, H2:]

    def weight_rows(zz, cc):
        s = 2 * zz + cc
        pg = contract_rows(X[:, s].reshape(E * T, S), GU[...])
        pd = contract_rows(Y[:, s].reshape(E * T, S), HD[...])
        for e in range(E):
            m = TM[e, pl.ds(s, 1), :]
            DW[s, e, :, :H] = (pg[:, e * H2 : e * H2 + H] * m).astype(BF16)
            DW[s, e, :, H:H2] = (pg[:, e * H2 + H : (e + 1) * H2] * m).astype(BF16)
            DW[s, e, :, H2:] = (pd[:, e * H : (e + 1) * H] * m).astype(BF16)

    def sib_copy(zz):
        return rcopy(DW.at[2 * zz + 1 - c], SB.at[zz], bs.at[zz], br.at[zz], sib)

    def up_copy(t):
        return rcopy(DW.at[2 * t + c], UP.at[t], us.at[0, t], ur.at[0, t], above)

    def dn_copy(t):
        return rcopy(DW.at[2 * t + c], DN.at[t], us.at[1, t], ur.at[1, t], below)

    order = []
    for i in range((Z + 1) // 2):
        order += [Z - 1 - i] + ([i] if i != Z - 1 - i else [])
    for t in order:
        weight_rows(t, 1 - c)
        sib_copy(t).start()
    for t in order:
        weight_rows(t, c)

    def send_grads(t):
        s = 2 * t + c
        sib_copy(t).wait_recv()

        @pl.when(t > z)
        def _():
            @pl.when(has_dn)
            def _():
                up_copy(t).wait_recv()
                DW[s] = (DW[s].astype(F32) + SB[t].astype(F32) + UP[t].astype(F32)).astype(BF16)

            @pl.when(z == 0)
            def _():
                DW[s] = (DW[s].astype(F32) + SB[t].astype(F32)).astype(BF16)

            up_copy(t).start()

        @pl.when(t < z)
        def _():
            @pl.when(has_up)
            def _():
                dn_copy(t).wait_recv()
                DW[s] = (DW[s].astype(F32) + SB[t].astype(F32) + DN[t].astype(F32)).astype(BF16)

            @pl.when(z == Z - 1)
            def _():
                DW[s] = (DW[s].astype(F32) + SB[t].astype(F32)).astype(BF16)

            dn_copy(t).start()

    def input_rows(s):
        tot = jnp.zeros((E * T, S), F32)
        for e in range(E):
            tot = tot + lax.dot_general(
                GU[:, e * H2 : (e + 1) * H2],
                W[s, e, :, :H2],
                (((1,), (1,)), ((), ())),
                preferred_element_type=F32,
            )
        DX[:, s] = tot.astype(BF16).reshape(E, T, S)

    for i, t in enumerate(order):
        send_grads(t)
        if i == 1 or Z == 1:
            def body(s, carry):
                input_rows(s)
                return carry

            lax.fori_loop(0, R, body, 0)
            for j in range(1, E):
                start(7, j, DX.at[peer(j)], dx_out.at[q])
            dx_out[q] = DX[q]

    for e in range(E):
        FS[e] = DW[r, e].astype(F32) + SB[z, e].astype(F32)

    @pl.when(has_dn)
    def _():
        up_copy(z).wait_recv()
        FS[...] += UP[z].astype(F32)

    @pl.when(has_up)
    def _():
        dn_copy(z).wait_recv()
        FS[...] += DN[z].astype(F32)

    for e in range(E):
        DW[r, e] = FS[e].astype(BF16)
    for j in range(1, E):
        start(8, j, DW.at[r, peer(j)], FW.at[q])
    dw_out[q] = FS[q]
    for j in range(1, E):
        got(8, j, FW)
        p = peer(j)
        dw_out[p] = FW[p].astype(F32)
    for j in range(1, E):
        got(7, j, dx_out)

    for d in sent:
        d.wait_send()
    for t in range(Z):
        w_sib(t).wait_send()
        sib_copy(t).wait_send()

        @pl.when((t <= z) & has_up)
        def _():
            w_up(t).wait_send()

        @pl.when((t >= z) & has_dn)
        def _():
            w_dn(t).wait_send()

        @pl.when(t > z)
        def _():
            up_copy(t).wait_send()

        @pl.when(t < z)
        def _():
            dn_copy(t).wait_send()


def by_width(tokens, grad_out, gates, expert_ids, w_all, touched):
    E, R = lax.axis_size("exp"), lax.axis_size("rep")
    T, D = tokens.shape
    S = D // (R * E)
    H = w_all.shape[2] // 3
    Z = R // 2

    def cut(a):
        return a.reshape(T, R, E, S).transpose(2, 1, 0, 3)

    w = w_all[0].reshape(E, S, 3 * H)
    ids = jnp.pad(expert_ids.astype(BF16), ((0, 0), (0, 128 - 2)))
    tm = jnp.broadcast_to(
        touched[0, 0].reshape(R, E).T.astype(F32)[:, :, None], (E, R, 128)
    )
    vm = pl.BlockSpec(memory_space=pltpu.VMEM)
    dma = pltpu.SemaphoreType.DMA
    dx, dw = pl.pallas_call(
        functools.partial(kernel, R, E, T, S, H),
        out_shape=(
            jax.ShapeDtypeStruct((E, R, T, S), BF16),
            jax.ShapeDtypeStruct((E, S, 3 * H), F32),
        ),
        in_specs=[vm] * 6,
        out_specs=(vm, vm),
        scratch_shapes=[
            pltpu.VMEM((E, R, T, S), BF16),
            pltpu.VMEM((E, R, T, S), BF16),
            pltpu.VMEM((E, T, 128), BF16),
            pltpu.VMEM((E, R, 128), F32),
            pltpu.VMEM((R, E, S, 3 * H), BF16),
            pltpu.VMEM((E * T, E * 3 * H), F32),
            pltpu.VMEM((E, T, 6 * H), BF16),
            pltpu.VMEM((E, T, 6 * H), BF16),
            pltpu.VMEM((E, T, 6 * H), BF16),
            pltpu.VMEM((E * T, E * 2 * H), BF16),
            pltpu.VMEM((E * T, E * H), BF16),
            pltpu.VMEM((E, R, T, S), BF16),
            pltpu.VMEM((R, E, S, 3 * H), BF16),
            pltpu.VMEM((Z, E, S, 3 * H), BF16),
            pltpu.VMEM((Z, E, S, 3 * H), BF16),
            pltpu.VMEM((Z, E, S, 3 * H), BF16),
            pltpu.VMEM((E, S, 3 * H), F32),
            pltpu.VMEM((E, S, 3 * H), BF16),
            dma((9, E)),
            dma((9, E)),
            dma((R,)),
            dma((3, Z)),
            dma((Z,)),
            dma((Z,)),
            dma((2, Z)),
            dma((2, Z)),
            dma((1,)),
        ],
        compiler_params=pltpu.CompilerParams(
            collective_id=0, has_side_effects=True, vmem_limit_bytes=52 * 1024 * 1024
        ),
    )(cut(tokens), cut(grad_out), w, ids, tm, gates)
    token_grad = dx.transpose(2, 1, 0, 3).reshape(T, D)
    return token_grad, dw.reshape(1, E * S, 3 * H)


def by_expert(tokens, grad_out, gates, expert_ids, w_all, touched):
    tok_count = tokens.shape[0]
    model_width = tokens.shape[1]
    expert_count = lax.axis_size("exp")
    capacity = 5 * tok_count // (2 * expert_count)
    slot_count = expert_count * capacity
    hidden_count = w_all.shape[2] // 3
    flat_ids = expert_ids.reshape(-1)
    onehot = (flat_ids[:, None] == jnp.arange(expert_count, dtype=jnp.int32)[None, :]).astype(
        jnp.int32
    )
    slot_rank = jnp.sum(jnp.cumsum(onehot, 0) * onehot, 1) - 1
    target = flat_ids * capacity + slot_rank
    placed = target[None, :] == jnp.arange(slot_count, dtype=jnp.int32)[:, None]
    place_pair = placed.astype(jnp.bfloat16)
    place_token = jnp.sum(placed.reshape(slot_count, tok_count, 2).astype(jnp.int32), 2).astype(
        jnp.bfloat16
    )
    scaled = (grad_out.astype(jnp.float32)[:, None, :] * gates[:, :, None]).astype(jnp.bfloat16)
    scaled = scaled.reshape(2 * tok_count, model_width)
    send_x = jnp.dot(place_token, tokens, preferred_element_type=jnp.float32).astype(jnp.bfloat16)
    send_dy = jnp.dot(place_pair, scaled, preferred_element_type=jnp.float32).astype(jnp.bfloat16)
    recv_x, recv_dy = (
        lax.all_to_all(
            send_x.reshape(expert_count, capacity, model_width),
            "exp",
            split_axis=0,
            concat_axis=0,
            tiled=True,
        ),
        lax.all_to_all(
            send_dy.reshape(expert_count, capacity, model_width),
            "exp",
            split_axis=0,
            concat_axis=0,
            tiled=True,
        ),
    )
    slot_x = recv_x.reshape(slot_count, model_width)
    slot_dy = recv_dy.reshape(slot_count, model_width)
    w_local = w_all[0]
    shard_rows = lax.all_gather(w_local, "rep", axis=0, tiled=True)
    gate_up = jnp.dot(slot_x, shard_rows[:, : 2 * hidden_count], preferred_element_type=jnp.float32)
    hid_grad = jnp.dot(
        slot_dy, shard_rows[:, 2 * hidden_count :], preferred_element_type=jnp.float32
    )
    gate_pre = gate_up[:, :hidden_count]
    up_pre = gate_up[:, hidden_count:]
    silu_val, silu_slope = silu_terms(gate_pre)
    hidden = (silu_val * up_pre).astype(jnp.bfloat16)
    gate_grad = (hid_grad * up_pre * silu_slope).astype(jnp.bfloat16)
    up_grad = (hid_grad * silu_val).astype(jnp.bfloat16)
    both_grad = jnp.concatenate([gate_grad, up_grad], 1)
    row_mask = jnp.repeat(touched[0, 0].astype(jnp.float32), 128)[:, None]
    full_grad = jnp.concatenate(
        [contract_rows(slot_x, both_grad), contract_rows(slot_dy, hidden)], 1
    )
    masked = lax.optimization_barrier((full_grad * row_mask).astype(jnp.bfloat16)).astype(
        jnp.float32
    )
    owned = lax.psum_scatter(
        masked.astype(jnp.bfloat16), "rep", scatter_dimension=0, tiled=True
    ).astype(jnp.float32)
    slot_grad = lax.dot_general(
        both_grad,
        shard_rows[:, : 2 * hidden_count],
        (((1,), (1,)), ((), ())),
        preferred_element_type=jnp.float32,
    )
    slot_grad = slot_grad.astype(jnp.bfloat16)
    returned = lax.all_to_all(
        slot_grad.reshape(expert_count, capacity, model_width),
        "exp",
        split_axis=0,
        concat_axis=0,
        tiled=True,
    )
    returned = returned.reshape(slot_count, model_width)
    token_grad = contract_rows(place_token, returned).astype(jnp.bfloat16)
    return (token_grad, owned[None])


def per_device(tokens, grad_out, gates, expert_ids, w_all, touched):
    R, E = lax.axis_size("rep"), lax.axis_size("exp")
    share, rest = divmod(tokens.shape[1], R * E)
    fits = rest == 0 and share == 128 and R % 16 in (0, 8)
    fits = fits and tokens.shape[0] % 16 == 0 and w_all.shape[2] == 3 * 128
    plan = by_width if fits else by_expert
    return plan(tokens, grad_out, gates, expert_ids, w_all, touched)


def solution(mesh):
    in_specs = (
        P(("rep", "exp"), None),
        P(("rep", "exp"), None),
        P(("rep", "exp"), None),
        P(("rep", "exp"), None),
        P("exp", "rep", None),
        P("rep", "exp", None),
    )
    out_specs = (P(("rep", "exp"), None), P("exp", "rep", None))
    return jax.shard_map(
        per_device, mesh=mesh, in_specs=in_specs, out_specs=out_specs, check_vma=False
    )
```

```python
import functools
import jax
import jax.numpy as jnp
from jax import lax
from jax.experimental import pallas as pl
from jax.experimental.pallas import tpu as pltpu
from jax.sharding import PartitionSpec as P

MESH = pl.DeviceIdType.MESH
BF16 = jnp.bfloat16
F32 = jnp.float32


def silu_terms(gate_pre):
    sigmoid_g = jax.nn.sigmoid(gate_pre)
    return (gate_pre * sigmoid_g, sigmoid_g * (1.0 + gate_pre * (1.0 - sigmoid_g)))


def contract_rows(left, right):
    return lax.dot_general(
        left, right, (((0,), (0,)), ((), ())), preferred_element_type=jnp.float32
    )


def kernel(
    R, E, T, S, H,
    x_ref, g_ref, w_ref, id_ref, tm_ref, gate_ref,
    dx_out, dw_out,
    X, Y, IDS, TM, WG, WD, CG, CD, PG, PD, QG, QD, AG, AD, GU, HD, DX,
    DG, DD, BG, BD, UG, UD, NG, ND, FG, FD, RG, RD,
    a2s, a2r, wr, ws, bs, br, us, ur, loc,
):
    H2 = 2 * H
    Z = R // 2
    r = lax.axis_index("rep")
    q = lax.axis_index("exp")
    z, c = r // 2, lax.rem(r, 2)
    sib = (2 * z + 1 - c, q)
    above = (lax.rem(r + 2, R), q)
    below = (lax.rem(r + R - 2, R), q)
    has_up, has_dn = z < Z - 1, z > 0

    def peer(j):
        return lax.rem(q + j, E)

    def span(s, p):
        return pl.ds(pl.multiple_of((s * E + p) * S, S), S)

    def own_cols(s, carry):
        pltpu.make_async_copy(x_ref.at[:, span(s, q)], X.at[q, s], loc.at[0]).start()
        pltpu.make_async_copy(g_ref.at[:, span(s, q)], Y.at[q, s], loc.at[1]).start()
        return carry

    lax.fori_loop(0, R, own_cols, 0)

    barrier = pltpu.get_barrier_semaphore()
    for j in range(1, E):
        pl.semaphore_signal(barrier, inc=1, device_id=(r, peer(j)), device_id_type=MESH)
    pl.semaphore_signal(barrier, inc=1, device_id=sib, device_id_type=MESH)

    @pl.when(has_up)
    def _():
        pl.semaphore_signal(barrier, inc=1, device_id=above, device_id_type=MESH)

    @pl.when(has_dn)
    def _():
        pl.semaphore_signal(barrier, inc=1, device_id=below, device_id_type=MESH)

    edge = jnp.where(z == 0, 1, 0) + jnp.where(z == Z - 1, 1, 0)
    pl.semaphore_wait(barrier, E + 2 - edge)

    def rcopy(src, dst, ss, rs, dev):
        return pltpu.make_async_remote_copy(
            src_ref=src, dst_ref=dst, send_sem=ss, recv_sem=rs, device_id=dev, device_id_type=MESH
        )

    sent = []

    def copy_to(kind, j, src, dst):
        return rcopy(src, dst, a2s.at[kind, j], a2r.at[kind, q], (r, peer(j)))

    def start(kind, j, src, dst):
        d = copy_to(kind, j, src, dst)
        d.start()
        sent.append(d)

    def got(kind, j, dst):
        p = peer(j)
        rcopy(dst, dst, a2s.at[kind, j], a2r.at[kind, p], (r, p)).wait_recv()

    for j in range(1, E):
        start(0, j, w_ref.at[peer(j), :, :H2], WG.at[r, q])
    for j in range(1, E):
        start(1, j, w_ref.at[peer(j), :, H2:], WD.at[r, q])
    for j in range(1, E):
        start(2, j, id_ref, IDS.at[q])
        start(3, j, tm_ref.at[peer(j)], TM.at[q])

    def send_cols(kind, src, buf):
        def body(s, carry):
            for j in range(1, E):
                copy_to(kind, j, src.at[:, span(s, peer(j))], buf.at[q, s]).start()
            return carry

        lax.fori_loop(0, R, body, 0)
        for j in range(1, E):
            sent.append(copy_to(kind, j, buf.at[q], buf.at[q]))

    send_cols(4, x_ref, X)
    send_cols(5, g_ref, Y)
    WG[r, q] = w_ref[q, :, :H2]
    WD[r, q] = w_ref[q, :, H2:]
    IDS[q] = id_ref[...]
    TM[q] = tm_ref[q]

    WP = (WG, WD)

    def w_copy(p, way, zz):
        s = 2 * zz + c
        dev = (above, below, sib)[way]
        return rcopy(WP[p].at[s], WP[p].at[s], ws.at[p, way, zz], wr.at[p, s], dev)

    def w_wait(p, s):
        rcopy(WP[p].at[s], WP[p].at[s], ws.at[p, 2, 0], wr.at[p, s], sib).wait_recv()

    def w_first(p):
        for j in range(1, E):
            got(p, j, WP[p].at[r, peer(j)])

        @pl.when(has_up)
        def _():
            w_copy(p, 0, z).start()

        @pl.when(has_dn)
        def _():
            w_copy(p, 1, z).start()

        w_copy(p, 2, z).start()

    def w_forward(p, d):
        lo, hi = z - d, z + d

        @pl.when(lo >= 0)
        def _():
            w_wait(p, 2 * lo + c)

            @pl.when(has_up)
            def _():
                w_copy(p, 0, lo).start()

            w_copy(p, 2, lo).start()

        @pl.when(hi < Z)
        def _():
            w_wait(p, 2 * hi + c)

            @pl.when(has_dn)
            def _():
                w_copy(p, 1, hi).start()

            w_copy(p, 2, hi).start()

    def project(p, s, first=False):
        src, wid, acc = ((X, H2, CG), (Y, H, CD))[p]
        rows = src[:, s].reshape(E * T, S)
        for e in range(E):
            v = jnp.dot(rows, WP[p][s, e], preferred_element_type=F32)
            if first:
                acc[:, e * wid : (e + 1) * wid] = v
            else:
                acc[:, e * wid : (e + 1) * wid] += v

    def project_at(p, d):
        if d == 0:
            project(p, r, True)
            w_wait(p, 2 * z + 1 - c)
            project(p, 2 * z + 1 - c)
            return
        for zz, there in ((z - d, z - d >= 0), (z + d, z + d < Z)):

            @pl.when(there)
            def _():
                project(p, 2 * zz + c)
                w_wait(p, 2 * zz + 1 - c)
                project(p, 2 * zz + 1 - c)

    w_first(0)
    w_first(1)
    for j in range(1, E):
        got(2, j, IDS.at[peer(j)])
        got(3, j, TM.at[peer(j)])
    if Z > 1:
        w_forward(0, 1)
        w_forward(1, 1)
    pltpu.make_async_copy(X.at[q], X.at[q], loc.at[0]).wait()
    for j in range(1, E):
        got(4, j, X.at[peer(j)])
    project_at(0, 0)
    if Z > 2:
        w_forward(0, 2)
    if Z > 1:
        project_at(0, 1)
    pltpu.make_async_copy(Y.at[q], Y.at[q], loc.at[1]).wait()
    for j in range(1, E):
        got(5, j, Y.at[peer(j)])
    if Z > 2:
        w_forward(1, 2)
    project_at(1, 0)
    if Z > 1:
        project_at(1, 1)
    for d in range(3, Z):
        w_forward(0, d)
        project_at(0, d - 1)
        if d < Z - 1:
            w_forward(1, d)
            project_at(1, d - 1)
    if Z > 2:
        project_at(0, Z - 1)

    def pairs(p):
        wid, acc, buf, dst = ((H2, CG, PG, QG), (H, CD, PD, QD))[p]
        for j in list(range(1, E)) + [0]:
            o = peer(j)
            ids = IDS[o].astype(F32)
            rows = pl.ds(pl.multiple_of(o * T, T), T)
            for k in range(2):
                tot = jnp.zeros((T, wid), F32)
                for e in range(E):
                    m = (ids[:, k : k + 1] == e).astype(F32)
                    tot = tot + m * acc[rows, e * wid : (e + 1) * wid]
                buf[o, :, k * wid : (k + 1) * wid] = tot.astype(BF16)
            if j:
                start(6 + p, j, buf.at[o], dst.at[q])

    def pair_sum(p, k):
        wid, buf, dst = ((H2, PG, QG), (H, PD, QD))[p]
        tot = buf[q, :, k * wid : (k + 1) * wid].astype(F32)
        for j in range(1, E):
            tot = tot + dst[peer(j), :, k * wid : (k + 1) * wid].astype(F32)
        return tot

    pairs(0)
    if Z > 3:
        w_forward(1, Z - 1)
        project_at(1, Z - 2)
    if Z > 2:
        project_at(1, Z - 1)
    pairs(1)
    for j in range(1, E):
        got(6, j, QG.at[peer(j)])
    acts = []
    for k in range(2):
        tot = pair_sum(0, k)
        silu_val, silu_slope = silu_terms(tot[:, :H])
        up_pre, gate = tot[:, H:], gate_ref[:, k : k + 1]
        acts.append((gate * up_pre * silu_slope, gate * silu_val))
        AD[q, :, k * H : (k + 1) * H] = (gate * (silu_val * up_pre)).astype(BF16)
    for j in range(1, E):
        start(8, j, AD.at[q], AD.at[q])
    for j in range(1, E):
        got(7, j, QD.at[peer(j)])
    for k in range(2):
        hid_grad = pair_sum(1, k)
        AG[q, :, k * H2 : k * H2 + H] = (hid_grad * acts[k][0]).astype(BF16)
        AG[q, :, k * H2 + H : (k + 1) * H2] = (hid_grad * acts[k][1]).astype(BF16)
    for j in range(1, E):
        start(9, j, AG.at[q], AG.at[q])

    def spread(p):
        wid, src, dst = ((H2, AG, GU), (H, AD, HD))[p]
        for j in range(E):
            o = peer(j)
            if j:
                got(9 - p, j, src.at[o])
            ids = IDS[o].astype(F32)
            rows = pl.ds(pl.multiple_of(o * T, T), T)
            a0 = src[o, :, :wid].astype(F32)
            a1 = src[o, :, wid:].astype(F32)
            for e in range(E):
                m0 = (ids[:, 0:1] == e).astype(F32)
                m1 = (ids[:, 1:2] == e).astype(F32)
                dst[rows, e * wid : (e + 1) * wid] = (m0 * a0 + m1 * a1).astype(BF16)

    DP, BP, UP, NP = (DG, DD), (BG, BD), (UG, UD), (NG, ND)

    def weight_rows(p, s):
        src, wid, act = ((X, H2, GU), (Y, H, HD))[p]
        v = contract_rows(src[:, s].reshape(E * T, S), act[...])
        for e in range(E):
            m = TM[e, pl.ds(s, 1), :]
            for h in range(0, wid, H):
                DP[p][s, e, :, h : h + H] = (v[:, e * wid + h : e * wid + h + H] * m).astype(BF16)

    def sib_copy(p, t):
        return rcopy(DP[p].at[2 * t + 1 - c], BP[p].at[t], bs.at[p, t], br.at[p, t], sib)

    def up_copy(p, t):
        return rcopy(DP[p].at[2 * t + c], UP[p].at[t], us.at[p, 0, t], ur.at[p, 0, t], above)

    def dn_copy(p, t):
        return rcopy(DP[p].at[2 * t + c], NP[p].at[t], us.at[p, 1, t], ur.at[p, 1, t], below)

    def grads(p, i):
        t = jnp.where(z < (Z + 1) // 2, Z - 1 - i, i)
        weight_rows(p, 2 * t + 1 - c)
        sib_copy(p, t).start()
        weight_rows(p, 2 * t + c)

    def add_in(p, t, others):
        s = 2 * t + c
        for e in range(E):
            tot = DP[p][s, e].astype(F32)
            for o in others:
                tot = tot + o[t, e].astype(F32)
            DP[p][s, e] = tot.astype(BF16)

    def chain(p, n):
        @pl.when(n >= z)
        def _():
            t = Z - 1 + z - n
            sib_copy(p, t).wait_recv()

            @pl.when(has_dn)
            def _():
                up_copy(p, t).wait_recv()
                add_in(p, t, (BP[p], UP[p]))

            @pl.when(z == 0)
            def _():
                add_in(p, t, (BP[p],))

            up_copy(p, t).start()

        @pl.when(n >= Z - 1 - z)
        def _():
            t = n - (Z - 1 - z)
            sib_copy(p, t).wait_recv()

            @pl.when(has_up)
            def _():
                dn_copy(p, t).wait_recv()
                add_in(p, t, (BP[p], NP[p]))

            @pl.when(z == Z - 1)
            def _():
                add_in(p, t, (BP[p],))

            dn_copy(p, t).start()

    def finish(p):
        fs, fin = ((FG, RG), (FD, RD))[p]
        sib_copy(p, z).wait_recv()
        for e in range(E):
            fs[e] = DP[p][r, e].astype(F32) + BP[p][z, e].astype(F32)

        @pl.when(has_dn)
        def _():
            up_copy(p, z).wait_recv()
            fs[...] += UP[p][z].astype(F32)

        @pl.when(has_up)
        def _():
            dn_copy(p, z).wait_recv()
            fs[...] += NP[p][z].astype(F32)

        for e in range(E):
            DP[p][r, e] = fs[e].astype(BF16)
        for j in range(1, E):
            start(12 - p, j, DP[p].at[r, peer(j)], fin.at[q])

    def place(p):
        cols, fs, fin = ((slice(0, H2), FG, RG), (slice(H2, 3 * H), FD, RD))[p]
        dw_out[q, :, cols] = fs[q]
        for j in range(1, E):
            got(12 - p, j, fin.at[peer(j)])
            dw_out[peer(j), :, cols] = fin[peer(j)].astype(F32)

    def input_rows(s, carry):
        tot = jnp.zeros((E * T, S), F32)
        for e in range(E):
            tot = tot + lax.dot_general(
                GU[:, e * H2 : (e + 1) * H2],
                WG[s, e],
                (((1,), (1,)), ((), ())),
                preferred_element_type=F32,
            )
        DX[:, s] = tot.astype(BF16).reshape(E, T, S)
        for j in range(1, E):
            copy_to(10, j, DX.at[peer(j), s], dx_out.at[:, span(s, q)]).start()
        dx_out[:, span(s, q)] = DX[q, s]
        return carry

    spread(1)
    for i in range(Z):
        grads(1, i)
    if Z > 1:
        chain(1, 0)
    spread(0)
    for i in range(Z):
        grads(0, i)
        if i == min(1, Z - 1) and Z > 2:
            chain(1, 1)
    if Z > 1:
        chain(0, 0)
    for n in range(2, Z - 1):
        chain(1, n)
        if n < Z - 2:
            chain(0, n - 1)
    lax.fori_loop(0, R, input_rows, 0)
    for j in range(1, E):
        sent.append(copy_to(10, j, DX.at[q], DX.at[q]))
    for n in range(max(1, Z - 3), Z - 1):
        chain(0, n)
    finish(1)
    finish(0)
    place(1)
    place(0)
    for j in range(1, E):
        got(10, j, DX.at[peer(j)])

    for d in sent:
        d.wait_send()
    for p in range(2):
        for t in range(Z):
            w_copy(p, 2, t).wait_send()
            sib_copy(p, t).wait_send()

            @pl.when((t <= z) & has_up)
            def _():
                w_copy(p, 0, t).wait_send()

            @pl.when((t >= z) & has_dn)
            def _():
                w_copy(p, 1, t).wait_send()

            @pl.when(t > z)
            def _():
                up_copy(p, t).wait_send()

            @pl.when(t < z)
            def _():
                dn_copy(p, t).wait_send()


def by_width(tokens, grad_out, gates, expert_ids, w_all, touched):
    E, R = lax.axis_size("exp"), lax.axis_size("rep")
    T, D = tokens.shape
    S = D // (R * E)
    H = w_all.shape[2] // 3
    Z = R // 2
    w = w_all[0].reshape(E, S, 3 * H)
    ids = jnp.pad(expert_ids.astype(BF16), ((0, 0), (0, 128 - 2)))
    tm = jnp.broadcast_to(
        touched[0, 0].reshape(R, E).T.astype(F32)[:, :, None], (E, R, 128)
    )
    vm = pl.BlockSpec(memory_space=pltpu.VMEM)
    hbm = pl.BlockSpec(memory_space=pl.ANY)
    dma = pltpu.SemaphoreType.DMA

    def two(*lead, kind=BF16, times=1):
        return [pltpu.VMEM(lead + (times * 2 * H,), kind), pltpu.VMEM(lead + (times * H,), kind)]

    wide = pltpu.VMEM((E, R, T, S), BF16)
    dx, dw = pl.pallas_call(
        functools.partial(kernel, R, E, T, S, H),
        out_shape=(
            jax.ShapeDtypeStruct((T, D), BF16),
            jax.ShapeDtypeStruct((E, S, 3 * H), F32),
        ),
        in_specs=[hbm] * 2 + [vm] * 4,
        out_specs=(vm, vm),
        scratch_shapes=[wide, wide, pltpu.VMEM((E, T, 128), BF16), pltpu.VMEM((E, R, 128), F32)]
        + two(R, E, S)
        + two(E * T, kind=F32, times=E)
        + two(E, T, times=2)
        + two(E, T, times=2)
        + two(E, T, times=2)
        + two(E * T, times=E)
        + [wide]
        + two(R, E, S)
        + two(Z, E, S)
        + two(Z, E, S)
        + two(Z, E, S)
        + two(E, S, kind=F32)
        + two(E, S)
        + [
            dma((13, E)),
            dma((13, E)),
            dma((2, R)),
            dma((2, 3, Z)),
            dma((2, Z)),
            dma((2, Z)),
            dma((2, 2, Z)),
            dma((2, 2, Z)),
            dma((2,)),
        ],
        compiler_params=pltpu.CompilerParams(
            collective_id=0, has_side_effects=True, vmem_limit_bytes=52 * 1024 * 1024
        ),
    )(tokens, grad_out, w, ids, tm, gates)
    return dx, dw.reshape(1, E * S, 3 * H)


def by_expert(tokens, grad_out, gates, expert_ids, w_all, touched):
    tok_count = tokens.shape[0]
    model_width = tokens.shape[1]
    expert_count = lax.axis_size("exp")
    capacity = 5 * tok_count // (2 * expert_count)
    slot_count = expert_count * capacity
    hidden_count = w_all.shape[2] // 3
    flat_ids = expert_ids.reshape(-1)
    onehot = (flat_ids[:, None] == jnp.arange(expert_count, dtype=jnp.int32)[None, :]).astype(
        jnp.int32
    )
    slot_rank = jnp.sum(jnp.cumsum(onehot, 0) * onehot, 1) - 1
    target = flat_ids * capacity + slot_rank
    placed = target[None, :] == jnp.arange(slot_count, dtype=jnp.int32)[:, None]
    place_pair = placed.astype(jnp.bfloat16)
    place_token = jnp.sum(placed.reshape(slot_count, tok_count, 2).astype(jnp.int32), 2).astype(
        jnp.bfloat16
    )
    scaled = (grad_out.astype(jnp.float32)[:, None, :] * gates[:, :, None]).astype(jnp.bfloat16)
    scaled = scaled.reshape(2 * tok_count, model_width)
    send_x = jnp.dot(place_token, tokens, preferred_element_type=jnp.float32).astype(jnp.bfloat16)
    send_dy = jnp.dot(place_pair, scaled, preferred_element_type=jnp.float32).astype(jnp.bfloat16)
    recv_x, recv_dy = (
        lax.all_to_all(
            send_x.reshape(expert_count, capacity, model_width),
            "exp",
            split_axis=0,
            concat_axis=0,
            tiled=True,
        ),
        lax.all_to_all(
            send_dy.reshape(expert_count, capacity, model_width),
            "exp",
            split_axis=0,
            concat_axis=0,
            tiled=True,
        ),
    )
    slot_x = recv_x.reshape(slot_count, model_width)
    slot_dy = recv_dy.reshape(slot_count, model_width)
    w_local = w_all[0]
    shard_rows = lax.all_gather(w_local, "rep", axis=0, tiled=True)
    gate_up = jnp.dot(slot_x, shard_rows[:, : 2 * hidden_count], preferred_element_type=jnp.float32)
    hid_grad = jnp.dot(
        slot_dy, shard_rows[:, 2 * hidden_count :], preferred_element_type=jnp.float32
    )
    gate_pre = gate_up[:, :hidden_count]
    up_pre = gate_up[:, hidden_count:]
    silu_val, silu_slope = silu_terms(gate_pre)
    hidden = (silu_val * up_pre).astype(jnp.bfloat16)
    gate_grad = (hid_grad * up_pre * silu_slope).astype(jnp.bfloat16)
    up_grad = (hid_grad * silu_val).astype(jnp.bfloat16)
    both_grad = jnp.concatenate([gate_grad, up_grad], 1)
    row_mask = jnp.repeat(touched[0, 0].astype(jnp.float32), 128)[:, None]
    full_grad = jnp.concatenate(
        [contract_rows(slot_x, both_grad), contract_rows(slot_dy, hidden)], 1
    )
    masked = lax.optimization_barrier((full_grad * row_mask).astype(jnp.bfloat16)).astype(
        jnp.float32
    )
    owned = lax.psum_scatter(
        masked.astype(jnp.bfloat16), "rep", scatter_dimension=0, tiled=True
    ).astype(jnp.float32)
    slot_grad = lax.dot_general(
        both_grad,
        shard_rows[:, : 2 * hidden_count],
        (((1,), (1,)), ((), ())),
        preferred_element_type=jnp.float32,
    )
    slot_grad = slot_grad.astype(jnp.bfloat16)
    returned = lax.all_to_all(
        slot_grad.reshape(expert_count, capacity, model_width),
        "exp",
        split_axis=0,
        concat_axis=0,
        tiled=True,
    )
    returned = returned.reshape(slot_count, model_width)
    token_grad = contract_rows(place_token, returned).astype(jnp.bfloat16)
    return (token_grad, owned[None])


def per_device(tokens, grad_out, gates, expert_ids, w_all, touched):
    R, E = lax.axis_size("rep"), lax.axis_size("exp")
    share, rest = divmod(tokens.shape[1], R * E)
    fits = rest == 0 and share == 128 and R % 16 in (0, 8)
    fits = fits and tokens.shape[0] % 16 == 0 and w_all.shape[2] == 3 * 128
    plan = by_width if fits else by_expert
    return plan(tokens, grad_out, gates, expert_ids, w_all, touched)


def solution(mesh):
    in_specs = (
        P(("rep", "exp"), None),
        P(("rep", "exp"), None),
        P(("rep", "exp"), None),
        P(("rep", "exp"), None),
        P("exp", "rep", None),
        P("rep", "exp", None),
    )
    out_specs = (P(("rep", "exp"), None), P("exp", "rep", None))
    return jax.shard_map(
        per_device, mesh=mesh, in_specs=in_specs, out_specs=out_specs, check_vma=False
    )
```

```python
import functools
import jax
import jax.numpy as jnp
from jax import lax
from jax.experimental import pallas as pl
from jax.experimental.pallas import tpu as pltpu
from jax.sharding import PartitionSpec as P

MESH = pl.DeviceIdType.MESH
BF16 = jnp.bfloat16
F32 = jnp.float32


def silu_terms(gate_pre):
    sigmoid_g = jax.nn.sigmoid(gate_pre)
    return (gate_pre * sigmoid_g, sigmoid_g * (1.0 + gate_pre * (1.0 - sigmoid_g)))


def contract_rows(left, right):
    return lax.dot_general(
        left, right, (((0,), (0,)), ((), ())), preferred_element_type=jnp.float32
    )


def kernel(
    R, E, T, S, H,
    x_ref, g_ref, w_ref, id_ref, tm_ref, gate_ref,
    dx_out, dw_out,
    X, Y, IDS, TM, WG, WD, CG, CD, PG, PD, QG, QD, AG, AD, GU, HD, DX,
    DG, DD, BG, BD, UG, UD, NG, ND, FG, FD, RG, RD,
    a2s, a2r, wr, ws, bs, br, us, ur, loc,
):
    H2 = 2 * H
    Z = R // 2
    r = lax.axis_index("rep")
    q = lax.axis_index("exp")
    z, c = r // 2, lax.rem(r, 2)
    sib = (2 * z + 1 - c, q)
    above = (lax.rem(r + 2, R), q)
    below = (lax.rem(r + R - 2, R), q)
    has_up, has_dn = z < Z - 1, z > 0

    def peer(j):
        return lax.rem(q + j, E)

    def span(s, p):
        return pl.ds(pl.multiple_of((s * E + p) * S, S), S)

    def own_cols(s, carry):
        pltpu.make_async_copy(x_ref.at[:, span(s, q)], X.at[q, s], loc.at[0]).start()
        pltpu.make_async_copy(g_ref.at[:, span(s, q)], Y.at[q, s], loc.at[1]).start()
        return carry

    pltpu.make_async_copy(w_ref.at[q, :, :H2], WG.at[r, q], loc.at[2]).start()
    pltpu.make_async_copy(w_ref.at[q, :, H2:], WD.at[r, q], loc.at[3]).start()
    lax.fori_loop(0, R, own_cols, 0)

    barrier = pltpu.get_barrier_semaphore()
    for j in range(1, E):
        pl.semaphore_signal(barrier, inc=1, device_id=(r, peer(j)), device_id_type=MESH)
    pl.semaphore_signal(barrier, inc=1, device_id=sib, device_id_type=MESH)

    @pl.when(has_up)
    def _():
        pl.semaphore_signal(barrier, inc=1, device_id=above, device_id_type=MESH)

    @pl.when(has_dn)
    def _():
        pl.semaphore_signal(barrier, inc=1, device_id=below, device_id_type=MESH)

    edge = jnp.where(z == 0, 1, 0) + jnp.where(z == Z - 1, 1, 0)
    pl.semaphore_wait(barrier, E + 2 - edge)

    def rcopy(src, dst, ss, rs, dev):
        return pltpu.make_async_remote_copy(
            src_ref=src, dst_ref=dst, send_sem=ss, recv_sem=rs, device_id=dev, device_id_type=MESH
        )

    sent = []

    def copy_to(kind, j, src, dst):
        return rcopy(src, dst, a2s.at[kind, j], a2r.at[kind, q], (r, peer(j)))

    def start(kind, j, src, dst):
        d = copy_to(kind, j, src, dst)
        d.start()
        sent.append(d)

    def got(kind, j, dst):
        p = peer(j)
        rcopy(dst, dst, a2s.at[kind, j], a2r.at[kind, p], (r, p)).wait_recv()

    WP = (WG, WD)

    def w_copy(p, way, zz, e):
        s = 2 * zz + c
        dev = (above, below, sib)[way]
        ref = WP[p].at[s, e]
        return rcopy(ref, ref, ws.at[p, way, zz, e], wr.at[p, s, e], dev)

    def w_wait(p, s, e):
        ref = WP[p].at[s, e]
        rcopy(ref, ref, ws.at[p, 2, 0, e], wr.at[p, s, e], sib).wait_recv()

    def w_slot(p, s):
        for j in range(E):
            w_wait(p, s, peer(j))

    def w_send(p, e):
        @pl.when(has_up)
        def _():
            w_copy(p, 0, z, e).start()

        @pl.when(has_dn)
        def _():
            w_copy(p, 1, z, e).start()

        w_copy(p, 2, z, e).start()

    def w_own(p):
        w_send(p, q)

    def w_first(p):
        for j in range(1, E):
            got(p, j, WP[p].at[r, peer(j)])
            w_send(p, peer(j))

    def w_forward(p, d):
        lo, hi = z - d, z + d

        def body(j, carry):
            e = lax.rem(q + j, E)

            @pl.when(lo >= 0)
            def _():
                w_wait(p, 2 * lo + c, e)

                @pl.when(has_up)
                def _():
                    w_copy(p, 0, lo, e).start()

                w_copy(p, 2, lo, e).start()

            @pl.when(hi < Z)
            def _():
                w_wait(p, 2 * hi + c, e)

                @pl.when(has_dn)
                def _():
                    w_copy(p, 1, hi, e).start()

                w_copy(p, 2, hi, e).start()

            return carry

        lax.fori_loop(0, E, body, 0)

    for j in range(1, E):
        start(0, j, w_ref.at[peer(j), :, :H2], WG.at[r, q])
    own_w = (
        pltpu.make_async_copy(w_ref.at[q, :, :H2], WG.at[r, q], loc.at[2]),
        pltpu.make_async_copy(w_ref.at[q, :, H2:], WD.at[r, q], loc.at[3]),
    )
    own_w[0].wait()
    w_own(0)
    for j in range(1, E):
        start(1, j, w_ref.at[peer(j), :, H2:], WD.at[r, q])
    own_w[1].wait()
    w_own(1)
    for j in range(1, E):
        start(2, j, id_ref, IDS.at[q])
        start(3, j, tm_ref.at[peer(j)], TM.at[q])

    def send_cols(kind, src, buf):
        def body(s, carry):
            for j in range(1, E):
                copy_to(kind, j, src.at[:, span(s, peer(j))], buf.at[q, s]).start()
            return carry

        lax.fori_loop(0, R, body, 0)
        for j in range(1, E):
            sent.append(copy_to(kind, j, buf.at[q], buf.at[q]))

    send_cols(4, x_ref, X)
    send_cols(5, g_ref, Y)
    IDS[q] = id_ref[...]
    TM[q] = tm_ref[q]

    def project(p, s, first=False):
        src, wid, acc = ((X, H2, CG), (Y, H, CD))[p]
        rows = src[:, s].reshape(E * T, S)
        for e in range(E):
            v = jnp.dot(rows, WP[p][s, e], preferred_element_type=F32)
            if first:
                acc[:, e * wid : (e + 1) * wid] = v
            else:
                acc[:, e * wid : (e + 1) * wid] += v

    def project_at(p, d):
        if d == 0:
            project(p, r, True)
            w_slot(p, 2 * z + 1 - c)
            project(p, 2 * z + 1 - c)
            return
        for zz, there in ((z - d, z - d >= 0), (z + d, z + d < Z)):

            @pl.when(there)
            def _():
                project(p, 2 * zz + c)
                w_slot(p, 2 * zz + 1 - c)
                project(p, 2 * zz + 1 - c)

    w_first(0)
    w_first(1)
    for j in range(1, E):
        got(2, j, IDS.at[peer(j)])
        got(3, j, TM.at[peer(j)])
    if Z > 1:
        w_forward(0, 1)
        w_forward(1, 1)
    pltpu.make_async_copy(X.at[q], X.at[q], loc.at[0]).wait()
    for j in range(1, E):
        got(4, j, X.at[peer(j)])
    project_at(0, 0)
    for d in range(2, Z):
        w_forward(0, d)
        project_at(0, d - 1)
        if d < Z - 1:
            w_forward(1, d)
    if Z > 1:
        project_at(0, Z - 1)

    def pairs(p):
        wid, acc, buf, dst = ((H2, CG, PG, QG), (H, CD, PD, QD))[p]
        for j in list(range(1, E)) + [0]:
            o = peer(j)
            ids = IDS[o].astype(F32)
            rows = pl.ds(pl.multiple_of(o * T, T), T)
            for k in range(2):
                tot = jnp.zeros((T, wid), F32)
                for e in range(E):
                    m = (ids[:, k : k + 1] == e).astype(F32)
                    tot = tot + m * acc[rows, e * wid : (e + 1) * wid]
                buf[o, :, k * wid : (k + 1) * wid] = tot.astype(BF16)
            if j:
                start(6 + p, j, buf.at[o], dst.at[q])

    def pair_sum(p, k):
        wid, buf, dst = ((H2, PG, QG), (H, PD, QD))[p]
        tot = buf[q, :, k * wid : (k + 1) * wid].astype(F32)
        for j in range(1, E):
            tot = tot + dst[peer(j), :, k * wid : (k + 1) * wid].astype(F32)
        return tot

    pairs(0)
    pltpu.make_async_copy(Y.at[q], Y.at[q], loc.at[1]).wait()
    for j in range(1, E):
        got(5, j, Y.at[peer(j)])
    for d in range(Z - 1):
        project_at(1, d)
    if Z > 2:
        w_forward(1, Z - 1)
    project_at(1, Z - 1)
    pairs(1)
    for j in range(1, E):
        got(6, j, QG.at[peer(j)])
    acts = []
    for k in range(2):
        tot = pair_sum(0, k)
        silu_val, silu_slope = silu_terms(tot[:, :H])
        up_pre, gate = tot[:, H:], gate_ref[:, k : k + 1]
        acts.append((gate * up_pre * silu_slope, gate * silu_val))
        AD[q, :, k * H : (k + 1) * H] = (gate * (silu_val * up_pre)).astype(BF16)
    for j in range(1, E):
        start(8, j, AD.at[q], AD.at[q])
    for j in range(1, E):
        got(7, j, QD.at[peer(j)])
    for k in range(2):
        hid_grad = pair_sum(1, k)
        AG[q, :, k * H2 : k * H2 + H] = (hid_grad * acts[k][0]).astype(BF16)
        AG[q, :, k * H2 + H : (k + 1) * H2] = (hid_grad * acts[k][1]).astype(BF16)
    for j in range(1, E):
        start(9, j, AG.at[q], AG.at[q])

    def spread(p):
        wid, src, dst = ((H2, AG, GU), (H, AD, HD))[p]
        for j in range(E):
            o = peer(j)
            if j:
                got(9 - p, j, src.at[o])
            ids = IDS[o].astype(F32)
            rows = pl.ds(pl.multiple_of(o * T, T), T)
            a0 = src[o, :, :wid].astype(F32)
            a1 = src[o, :, wid:].astype(F32)
            for e in range(E):
                m0 = (ids[:, 0:1] == e).astype(F32)
                m1 = (ids[:, 1:2] == e).astype(F32)
                dst[rows, e * wid : (e + 1) * wid] = (m0 * a0 + m1 * a1).astype(BF16)

    DP, BP, UP, NP = (DG, DD), (BG, BD), (UG, UD), (NG, ND)

    def weight_rows(p, s):
        src, wid, act = ((X, H2, GU), (Y, H, HD))[p]
        v = contract_rows(src[:, s].reshape(E * T, S), act[...])
        for e in range(E):
            m = TM[e, pl.ds(s, 1), :]
            for h in range(0, wid, H):
                DP[p][s, e, :, h : h + H] = (v[:, e * wid + h : e * wid + h + H] * m).astype(BF16)

    def sib_copy(p, t):
        return rcopy(DP[p].at[2 * t + 1 - c], BP[p].at[t], bs.at[p, t], br.at[p, t], sib)

    def up_copy(p, t, e):
        src = DP[p].at[2 * t + c, e]
        return rcopy(src, UP[p].at[t, e], us.at[p, 0, t, e], ur.at[p, 0, t, e], above)

    def dn_copy(p, t, e):
        src = DP[p].at[2 * t + c, e]
        return rcopy(src, NP[p].at[t, e], us.at[p, 1, t, e], ur.at[p, 1, t, e], below)

    def grads(p, i):
        t = jnp.where(z < (Z + 1) // 2, Z - 1 - i, i)
        weight_rows(p, 2 * t + 1 - c)
        sib_copy(p, t).start()
        weight_rows(p, 2 * t + c)

    def add_in(p, t, e, others):
        tot = DP[p][2 * t + c, e].astype(F32)
        for o in others:
            tot = tot + o[t, e].astype(F32)
        DP[p][2 * t + c, e] = tot.astype(BF16)

    def chain_ends(p, n):
        def send(t, copy):
            sib_copy(p, t).wait_recv()

            def body(j, carry):
                e = lax.rem(q + j, E)
                add_in(p, t, e, (BP[p],))
                copy(p, t, e).start()
                return carry

            lax.fori_loop(1, E + 1, body, 0)

        @pl.when(z == 0)
        def _():
            send(Z - 1 - n, up_copy)

        @pl.when(z == Z - 1)
        def _():
            send(n, dn_copy)

    def chain(p, n):
        def send(t, copy, got_ref):
            sib_copy(p, t).wait_recv()

            def body(j, carry):
                e = lax.rem(q + j, E)
                copy(p, t, e).wait_recv()
                add_in(p, t, e, (BP[p], got_ref))
                copy(p, t, e).start()
                return carry

            lax.fori_loop(1, E + 1, body, 0)

        @pl.when((n >= z) & has_dn)
        def _():
            send(Z - 1 + z - n, up_copy, UP[p])

        @pl.when((n >= Z - 1 - z) & has_up)
        def _():
            send(n - (Z - 1 - z), dn_copy, NP[p])

    def finish(p):
        fs, fin = ((FG, RG), (FD, RD))[p]
        sib_copy(p, z).wait_recv()
        for j in list(range(1, E)) + [0]:
            e = peer(j)
            fs[e] = DP[p][r, e].astype(F32) + BP[p][z, e].astype(F32)

            @pl.when(has_dn)
            def _():
                up_copy(p, z, e).wait_recv()
                fs[e] += UP[p][z, e].astype(F32)

            @pl.when(has_up)
            def _():
                dn_copy(p, z, e).wait_recv()
                fs[e] += NP[p][z, e].astype(F32)

            if j:
                DP[p][r, e] = fs[e].astype(BF16)
                start(12 - p, j, DP[p].at[r, e], fin.at[q])

    def place(p):
        cols, fs, fin = ((slice(0, H2), FG, RG), (slice(H2, 3 * H), FD, RD))[p]
        dw_out[q, :, cols] = fs[q]
        for j in range(1, E):
            got(12 - p, j, fin.at[peer(j)])
            dw_out[peer(j), :, cols] = fin[peer(j)].astype(F32)

    def input_rows(s, carry):
        tot = jnp.zeros((E * T, S), F32)
        for e in range(E):
            tot = tot + lax.dot_general(
                GU[:, e * H2 : (e + 1) * H2],
                WG[s, e],
                (((1,), (1,)), ((), ())),
                preferred_element_type=F32,
            )
        DX[:, s] = tot.astype(BF16).reshape(E, T, S)
        for j in range(1, E):
            copy_to(10, j, DX.at[peer(j), s], dx_out.at[:, span(s, q)]).start()
        pltpu.make_async_copy(DX.at[q, s], dx_out.at[:, span(s, q)], loc.at[4]).start()
        return carry

    spread(1)
    for i in range(Z):
        grads(1, i)
        if i:
            chain_ends(1, i - 1)
    spread(0)
    for i in range(Z):
        grads(0, i)
        if i:
            chain_ends(0, i - 1)
        if i == Z // 2 and Z > 2:
            chain(1, 1)
    for n in range(2, Z - 1):
        chain(1, n)
        if n < Z - 2:
            chain(0, n - 1)
    if Z > 2:
        chain(0, max(1, Z - 3))
    lax.fori_loop(0, R, input_rows, 0)
    for j in range(1, E):
        sent.append(copy_to(10, j, DX.at[q], DX.at[q]))
    for n in range(max(1, Z - 3) + 1, Z - 1):
        chain(0, n)
    finish(1)
    finish(0)
    place(1)
    place(0)
    for j in range(1, E):
        got(10, j, DX.at[peer(j)])
    pltpu.make_async_copy(DX.at[q], DX.at[q], loc.at[4]).wait()

    for d in sent:
        d.wait_send()
    for p in range(2):
        for t in range(Z):
            sib_copy(p, t).wait_send()

            def left(e, carry):
                w_copy(p, 2, t, e).wait_send()

                @pl.when((t <= z) & has_up)
                def _():
                    w_copy(p, 0, t, e).wait_send()

                @pl.when((t >= z) & has_dn)
                def _():
                    w_copy(p, 1, t, e).wait_send()

                @pl.when(t > z)
                def _():
                    up_copy(p, t, e).wait_send()

                @pl.when(t < z)
                def _():
                    dn_copy(p, t, e).wait_send()

                return carry

            lax.fori_loop(0, E, left, 0)


def by_width(tokens, grad_out, gates, expert_ids, w_all, touched):
    E, R = lax.axis_size("exp"), lax.axis_size("rep")
    T, D = tokens.shape
    S = D // (R * E)
    H = w_all.shape[2] // 3
    Z = R // 2
    w = w_all[0].reshape(E, S, 3 * H)
    ids = jnp.pad(expert_ids.astype(BF16), ((0, 0), (0, 128 - 2)))
    tm = jnp.broadcast_to(
        touched[0, 0].reshape(R, E).T.astype(F32)[:, :, None], (E, R, 128)
    )
    vm = pl.BlockSpec(memory_space=pltpu.VMEM)
    hbm = pl.BlockSpec(memory_space=pltpu.HBM)
    dma = pltpu.SemaphoreType.DMA

    def two(*lead, kind=BF16, times=1):
        return [pltpu.VMEM(lead + (times * 2 * H,), kind), pltpu.VMEM(lead + (times * H,), kind)]

    wide = pltpu.VMEM((E, R, T, S), BF16)
    dx, dw = pl.pallas_call(
        functools.partial(kernel, R, E, T, S, H),
        out_shape=(
            jax.ShapeDtypeStruct((T, D), BF16),
            jax.ShapeDtypeStruct((E, S, 3 * H), F32),
        ),
        in_specs=[hbm] * 3 + [vm] * 3,
        out_specs=(hbm, vm),
        scratch_shapes=[wide, wide, pltpu.VMEM((E, T, 128), BF16), pltpu.VMEM((E, R, 128), F32)]
        + two(R, E, S)
        + two(E * T, kind=F32, times=E)
        + two(E, T, times=2)
        + two(E, T, times=2)
        + two(E, T, times=2)
        + two(E * T, times=E)
        + [wide]
        + two(R, E, S)
        + two(Z, E, S)
        + two(Z, E, S)
        + two(Z, E, S)
        + two(E, S, kind=F32)
        + two(E, S)
        + [
            dma((13, E)),
            dma((13, E)),
            dma((2, R, E)),
            dma((2, 3, Z, E)),
            dma((2, Z)),
            dma((2, Z)),
            dma((2, 2, Z, E)),
            dma((2, 2, Z, E)),
            dma((5,)),
        ],
        compiler_params=pltpu.CompilerParams(
            collective_id=0, has_side_effects=True, vmem_limit_bytes=52 * 1024 * 1024
        ),
    )(tokens, grad_out, w, ids, tm, gates)
    return dx, dw.reshape(1, E * S, 3 * H)


def by_expert(tokens, grad_out, gates, expert_ids, w_all, touched):
    tok_count = tokens.shape[0]
    model_width = tokens.shape[1]
    expert_count = lax.axis_size("exp")
    capacity = 5 * tok_count // (2 * expert_count)
    slot_count = expert_count * capacity
    hidden_count = w_all.shape[2] // 3
    flat_ids = expert_ids.reshape(-1)
    onehot = (flat_ids[:, None] == jnp.arange(expert_count, dtype=jnp.int32)[None, :]).astype(
        jnp.int32
    )
    slot_rank = jnp.sum(jnp.cumsum(onehot, 0) * onehot, 1) - 1
    target = flat_ids * capacity + slot_rank
    placed = target[None, :] == jnp.arange(slot_count, dtype=jnp.int32)[:, None]
    place_pair = placed.astype(jnp.bfloat16)
    place_token = jnp.sum(placed.reshape(slot_count, tok_count, 2).astype(jnp.int32), 2).astype(
        jnp.bfloat16
    )
    scaled = (grad_out.astype(jnp.float32)[:, None, :] * gates[:, :, None]).astype(jnp.bfloat16)
    scaled = scaled.reshape(2 * tok_count, model_width)
    send_x = jnp.dot(place_token, tokens, preferred_element_type=jnp.float32).astype(jnp.bfloat16)
    send_dy = jnp.dot(place_pair, scaled, preferred_element_type=jnp.float32).astype(jnp.bfloat16)
    recv_x, recv_dy = (
        lax.all_to_all(
            send_x.reshape(expert_count, capacity, model_width),
            "exp",
            split_axis=0,
            concat_axis=0,
            tiled=True,
        ),
        lax.all_to_all(
            send_dy.reshape(expert_count, capacity, model_width),
            "exp",
            split_axis=0,
            concat_axis=0,
            tiled=True,
        ),
    )
    slot_x = recv_x.reshape(slot_count, model_width)
    slot_dy = recv_dy.reshape(slot_count, model_width)
    w_local = w_all[0]
    shard_rows = lax.all_gather(w_local, "rep", axis=0, tiled=True)
    gate_up = jnp.dot(slot_x, shard_rows[:, : 2 * hidden_count], preferred_element_type=jnp.float32)
    hid_grad = jnp.dot(
        slot_dy, shard_rows[:, 2 * hidden_count :], preferred_element_type=jnp.float32
    )
    gate_pre = gate_up[:, :hidden_count]
    up_pre = gate_up[:, hidden_count:]
    silu_val, silu_slope = silu_terms(gate_pre)
    hidden = (silu_val * up_pre).astype(jnp.bfloat16)
    gate_grad = (hid_grad * up_pre * silu_slope).astype(jnp.bfloat16)
    up_grad = (hid_grad * silu_val).astype(jnp.bfloat16)
    both_grad = jnp.concatenate([gate_grad, up_grad], 1)
    row_mask = jnp.repeat(touched[0, 0].astype(jnp.float32), 128)[:, None]
    full_grad = jnp.concatenate(
        [contract_rows(slot_x, both_grad), contract_rows(slot_dy, hidden)], 1
    )
    masked = lax.optimization_barrier((full_grad * row_mask).astype(jnp.bfloat16)).astype(
        jnp.float32
    )
    owned = lax.psum_scatter(
        masked.astype(jnp.bfloat16), "rep", scatter_dimension=0, tiled=True
    ).astype(jnp.float32)
    slot_grad = lax.dot_general(
        both_grad,
        shard_rows[:, : 2 * hidden_count],
        (((1,), (1,)), ((), ())),
        preferred_element_type=jnp.float32,
    )
    slot_grad = slot_grad.astype(jnp.bfloat16)
    returned = lax.all_to_all(
        slot_grad.reshape(expert_count, capacity, model_width),
        "exp",
        split_axis=0,
        concat_axis=0,
        tiled=True,
    )
    returned = returned.reshape(slot_count, model_width)
    token_grad = contract_rows(place_token, returned).astype(jnp.bfloat16)
    return (token_grad, owned[None])


def per_device(tokens, grad_out, gates, expert_ids, w_all, touched):
    R, E = lax.axis_size("rep"), lax.axis_size("exp")
    share, rest = divmod(tokens.shape[1], R * E)
    fits = rest == 0 and share == 128 and R % 16 in (0, 8)
    fits = fits and tokens.shape[0] % 16 == 0 and w_all.shape[2] == 3 * 128
    plan = by_width if fits else by_expert
    return plan(tokens, grad_out, gates, expert_ids, w_all, touched)


def solution(mesh):
    in_specs = (
        P(("rep", "exp"), None),
        P(("rep", "exp"), None),
        P(("rep", "exp"), None),
        P(("rep", "exp"), None),
        P("exp", "rep", None),
        P("rep", "exp", None),
    )
    out_specs = (P(("rep", "exp"), None), P("exp", "rep", None))
    return jax.shard_map(
        per_device, mesh=mesh, in_specs=in_specs, out_specs=out_specs, check_vma=False
    )
```

```python
import functools
import jax
import jax.numpy as jnp
from jax import lax
from jax.experimental import pallas as pl
from jax.experimental.pallas import tpu as pltpu
from jax.sharding import PartitionSpec as P

MESH = pl.DeviceIdType.MESH
BF16 = jnp.bfloat16
F32 = jnp.float32


def silu_terms(gate_pre):
    sigmoid_g = jax.nn.sigmoid(gate_pre)
    return (gate_pre * sigmoid_g, sigmoid_g * (1.0 + gate_pre * (1.0 - sigmoid_g)))


def contract_rows(left, right):
    return lax.dot_general(
        left, right, (((0,), (0,)), ((), ())), preferred_element_type=jnp.float32
    )


def kernel(
    R, E, T, S, H,
    x_ref, g_ref, w_ref, id_ref, tm_ref, gate_ref,
    dx_out, dw_out,
    X, Y, XT, YT, IDS, TM, WG, WD, CG, CD, PG, PD, QG, QD, AG, AD, GU, HD, DX,
    DG, DD, BG, BD, UG, UD, NG, ND, FG, FD, RG, RD,
    a2s, a2r, wr, ws, bs, br, us, ur, loc,
):
    H2 = 2 * H
    Z = R // 2
    r = lax.axis_index("rep")
    q = lax.axis_index("exp")
    z, c = r // 2, lax.rem(r, 2)
    sib = (2 * z + 1 - c, q)
    above = (lax.rem(r + 2, R), q)
    below = (lax.rem(r + R - 2, R), q)
    has_up, has_dn = z < Z - 1, z > 0

    def peer(j):
        return lax.rem(q + j, E)

    def span(s, p):
        return pl.ds(pl.multiple_of((s * E + p) * S, S), S)

    def own_cols(s, carry):
        pltpu.make_async_copy(x_ref.at[:, span(s, q)], X.at[q, s], loc.at[0]).start()
        pltpu.make_async_copy(g_ref.at[:, span(s, q)], Y.at[q, s], loc.at[1]).start()
        return carry

    pltpu.make_async_copy(w_ref.at[q, :, :H2], WG.at[r, q], loc.at[2]).start()
    pltpu.make_async_copy(w_ref.at[q, :, H2:], WD.at[r, q], loc.at[3]).start()
    lax.fori_loop(0, R, own_cols, 0)

    barrier = pltpu.get_barrier_semaphore()
    for j in range(1, E):
        pl.semaphore_signal(barrier, inc=1, device_id=(r, peer(j)), device_id_type=MESH)
    pl.semaphore_signal(barrier, inc=1, device_id=sib, device_id_type=MESH)

    @pl.when(has_up)
    def _():
        pl.semaphore_signal(barrier, inc=1, device_id=above, device_id_type=MESH)

    @pl.when(has_dn)
    def _():
        pl.semaphore_signal(barrier, inc=1, device_id=below, device_id_type=MESH)

    edge = jnp.where(z == 0, 1, 0) + jnp.where(z == Z - 1, 1, 0)
    pl.semaphore_wait(barrier, E + 2 - edge)

    def rcopy(src, dst, ss, rs, dev):
        return pltpu.make_async_remote_copy(
            src_ref=src, dst_ref=dst, send_sem=ss, recv_sem=rs, device_id=dev, device_id_type=MESH
        )

    sent = []

    def copy_to(kind, j, src, dst):
        return rcopy(src, dst, a2s.at[kind, j], a2r.at[kind, q], (r, peer(j)))

    def start(kind, j, src, dst):
        d = copy_to(kind, j, src, dst)
        d.start()
        sent.append(d)

    def got(kind, j, dst):
        p = peer(j)
        rcopy(dst, dst, a2s.at[kind, j], a2r.at[kind, p], (r, p)).wait_recv()

    WP = (WG, WD)

    def w_copy(p, way, zz, e):
        s = 2 * zz + c
        dev = (above, below, sib)[way]
        ref = WP[p].at[s, e]
        return rcopy(ref, ref, ws.at[p, way, zz, e], wr.at[p, s, e], dev)

    def w_wait(p, s, e):
        ref = WP[p].at[s, e]
        rcopy(ref, ref, ws.at[p, 2, 0, e], wr.at[p, s, e], sib).wait_recv()

    def w_slot(p, s):
        for j in range(E):
            w_wait(p, s, peer(j))

    def w_send(p, e):
        @pl.when(has_up)
        def _():
            w_copy(p, 0, z, e).start()

        @pl.when(has_dn)
        def _():
            w_copy(p, 1, z, e).start()

        w_copy(p, 2, z, e).start()

    def w_own(p):
        w_send(p, q)

    def w_first(p):
        for j in range(1, E):
            got(p, j, WP[p].at[r, peer(j)])
            w_send(p, peer(j))

    def w_forward(p, d):
        lo, hi = z - d, z + d

        def body(j, carry):
            e = lax.rem(q + j, E)

            @pl.when(lo >= 0)
            def _():
                w_wait(p, 2 * lo + c, e)

                @pl.when(has_up)
                def _():
                    w_copy(p, 0, lo, e).start()

                w_copy(p, 2, lo, e).start()

            @pl.when(hi < Z)
            def _():
                w_wait(p, 2 * hi + c, e)

                @pl.when(has_dn)
                def _():
                    w_copy(p, 1, hi, e).start()

                w_copy(p, 2, hi, e).start()

            return carry

        lax.fori_loop(0, E, body, 0)

    for j in range(1, E):
        start(0, j, w_ref.at[peer(j), :, :H2], WG.at[r, q])
    own_w = (
        pltpu.make_async_copy(w_ref.at[q, :, :H2], WG.at[r, q], loc.at[2]),
        pltpu.make_async_copy(w_ref.at[q, :, H2:], WD.at[r, q], loc.at[3]),
    )
    own_w[0].wait()
    w_own(0)
    for j in range(1, E):
        start(1, j, w_ref.at[peer(j), :, H2:], WD.at[r, q])
    own_w[1].wait()
    w_own(1)
    for j in range(1, E):
        start(2, j, id_ref, IDS.at[q])
        start(3, j, tm_ref.at[peer(j)], TM.at[q])

    def send_cols(kind, src, buf):
        def body(s, carry):
            for j in range(1, E):
                copy_to(kind, j, src.at[:, span(s, peer(j))], buf.at[q, s]).start()
            return carry

        lax.fori_loop(0, R, body, 0)
        for j in range(1, E):
            sent.append(copy_to(kind, j, buf.at[q], buf.at[q]))

    send_cols(4, x_ref, X)
    send_cols(5, g_ref, Y)
    IDS[q] = id_ref[...]
    TM[q] = tm_ref[q]

    def project(p, s, first=False):
        src, wid, acc = ((X, H2, CG), (Y, H, CD))[p]
        rows = src[:, s].reshape(E * T, S)
        for e in range(E):
            v = jnp.dot(rows, WP[p][s, e], preferred_element_type=F32)
            if first:
                acc[:, e * wid : (e + 1) * wid] = v
            else:
                acc[:, e * wid : (e + 1) * wid] += v

    def project_at(p, d):
        if d == 0:
            project(p, r, True)
            w_slot(p, 2 * z + 1 - c)
            project(p, 2 * z + 1 - c)
            return
        for zz, there in ((z - d, z - d >= 0), (z + d, z + d < Z)):

            @pl.when(there)
            def _():
                project(p, 2 * zz + c)
                w_slot(p, 2 * zz + 1 - c)
                project(p, 2 * zz + 1 - c)

    def turn(src, dst):
        def body(s, carry):
            dst[s] = src[:, s].reshape(E * T, S).T
            return carry

        lax.fori_loop(0, R, body, 0)

    w_first(0)
    w_first(1)
    for j in range(1, E):
        got(2, j, IDS.at[peer(j)])
        got(3, j, TM.at[peer(j)])
    if Z > 1:
        w_forward(0, 1)
    pltpu.make_async_copy(X.at[q], X.at[q], loc.at[0]).wait()
    for j in range(1, E):
        got(4, j, X.at[peer(j)])
    for d in range(1, Z):
        if d > 1:
            w_forward(0, d)
        project_at(0, d - 1)
    project_at(0, Z - 1)

    def pairs(p):
        wid, acc, buf, dst = ((H2, CG, PG, QG), (H, CD, PD, QD))[p]
        for j in list(range(1, E)) + [0]:
            o = peer(j)
            ids = IDS[o].astype(F32)
            rows = pl.ds(pl.multiple_of(o * T, T), T)
            for k in range(2):
                tot = jnp.zeros((T, wid), F32)
                for e in range(E):
                    m = (ids[:, k : k + 1] == e).astype(F32)
                    tot = tot + m * acc[rows, e * wid : (e + 1) * wid]
                buf[o, :, k * wid : (k + 1) * wid] = tot.astype(BF16)
            if j:
                start(6 + p, j, buf.at[o], dst.at[q])

    def pair_sum(p, k):
        wid, buf, dst = ((H2, PG, QG), (H, PD, QD))[p]
        tot = buf[q, :, k * wid : (k + 1) * wid].astype(F32)
        for j in range(1, E):
            tot = tot + dst[peer(j), :, k * wid : (k + 1) * wid].astype(F32)
        return tot

    acts = []

    def hidden():
        for j in range(1, E):
            got(6, j, QG.at[peer(j)])
        for k in range(2):
            tot = pair_sum(0, k)
            silu_val, silu_slope = silu_terms(tot[:, :H])
            up_pre, gate = tot[:, H:], gate_ref[:, k : k + 1]
            acts.append((gate * up_pre * silu_slope, gate * silu_val))
            AD[q, :, k * H : (k + 1) * H] = (gate * (silu_val * up_pre)).astype(BF16)
        for j in range(1, E):
            start(8, j, AD.at[q], AD.at[q])

    def gate_up():
        for j in range(1, E):
            got(7, j, QD.at[peer(j)])
        for k in range(2):
            hid_grad = pair_sum(1, k)
            AG[q, :, k * H2 : k * H2 + H] = (hid_grad * acts[k][0]).astype(BF16)
            AG[q, :, k * H2 + H : (k + 1) * H2] = (hid_grad * acts[k][1]).astype(BF16)
        for j in range(1, E):
            start(9, j, AG.at[q], AG.at[q])

    pairs(0)
    if Z > 1:
        w_forward(1, 1)
    pltpu.make_async_copy(Y.at[q], Y.at[q], loc.at[1]).wait()
    for j in range(1, E):
        got(5, j, Y.at[peer(j)])
    project_at(1, 0)
    for d in range(2, Z):
        w_forward(1, d)
        if d == 2:
            turn(X, XT)
            turn(Y, YT)
        project_at(1, d - 1)
        if d == 2:
            hidden()
    if Z > 1:
        project_at(1, Z - 1)
    if Z <= 2:
        turn(X, XT)
        turn(Y, YT)
        hidden()
    pairs(1)

    def spread(p):
        wid, src, dst = ((H2, AG, GU), (H, AD, HD))[p]
        for j in range(E):
            o = peer(j)
            if j:
                got(9 - p, j, src.at[o])
            ids = IDS[o].astype(F32)
            rows = pl.ds(pl.multiple_of(o * T, T), T)
            a0 = src[o, :, :wid].astype(F32)
            a1 = src[o, :, wid:].astype(F32)
            for e in range(E):
                m0 = (ids[:, 0:1] == e).astype(F32)
                m1 = (ids[:, 1:2] == e).astype(F32)
                dst[rows, e * wid : (e + 1) * wid] = (m0 * a0 + m1 * a1).astype(BF16)

    DP, BP, UP, NP = (DG, DD), (BG, BD), (UG, UD), (NG, ND)

    def weight_rows(p, t):
        src, wid, act = ((XT, H2, GU), (YT, H, HD))[p]
        rows = src[pl.ds(2 * t, 2)].reshape(2 * S, E * T)
        step = min(E * wid, H2)
        for n in range(0, E * wid, step):
            v = jnp.dot(rows, act[:, n : n + step], preferred_element_type=F32)
            for h in range(n, n + step, H):
                e, col = h // wid, h % wid
                for half in range(2):
                    s = 2 * t + half
                    m = TM[e, pl.ds(s, 1), :]
                    part = v[half * S : (half + 1) * S, h - n : h - n + H]
                    DP[p][s, e, :, col : col + H] = (part * m).astype(BF16)

    def sib_copy(p, t):
        return rcopy(DP[p].at[2 * t + 1 - c], BP[p].at[t], bs.at[p, t], br.at[p, t], sib)

    def up_copy(p, t, e):
        src = DP[p].at[2 * t + c, e]
        return rcopy(src, UP[p].at[t, e], us.at[p, 0, t, e], ur.at[p, 0, t, e], above)

    def dn_copy(p, t, e):
        src = DP[p].at[2 * t + c, e]
        return rcopy(src, NP[p].at[t, e], us.at[p, 1, t, e], ur.at[p, 1, t, e], below)

    def grads(p, i):
        t = jnp.where(z < (Z + 1) // 2, Z - 1 - i, i)
        weight_rows(p, t)
        sib_copy(p, t).start()

    def add_in(p, t, e, others):
        tot = DP[p][2 * t + c, e].astype(F32)
        for o in others:
            tot = tot + o[t, e].astype(F32)
        DP[p][2 * t + c, e] = tot.astype(BF16)

    def chain_ends(p, n):
        def send(t, copy):
            sib_copy(p, t).wait_recv()

            def body(j, carry):
                e = lax.rem(q + j, E)
                add_in(p, t, e, (BP[p],))
                copy(p, t, e).start()
                return carry

            lax.fori_loop(1, E + 1, body, 0)

        @pl.when(z == 0)
        def _():
            send(Z - 1 - n, up_copy)

        @pl.when(z == Z - 1)
        def _():
            send(n, dn_copy)

    def chain(p, n):
        def send(t, copy, got_ref):
            sib_copy(p, t).wait_recv()

            def body(j, carry):
                e = lax.rem(q + j, E)
                copy(p, t, e).wait_recv()
                add_in(p, t, e, (BP[p], got_ref))
                copy(p, t, e).start()
                return carry

            lax.fori_loop(1, E + 1, body, 0)

        @pl.when((n >= z) & has_dn)
        def _():
            send(Z - 1 + z - n, up_copy, UP[p])

        @pl.when((n >= Z - 1 - z) & has_up)
        def _():
            send(n - (Z - 1 - z), dn_copy, NP[p])

    def finish(p):
        fs, fin = ((FG, RG), (FD, RD))[p]
        sib_copy(p, z).wait_recv()
        for j in list(range(1, E)) + [0]:
            e = peer(j)
            fs[e] = DP[p][r, e].astype(F32) + BP[p][z, e].astype(F32)

            @pl.when(has_dn)
            def _():
                up_copy(p, z, e).wait_recv()
                fs[e] += UP[p][z, e].astype(F32)

            @pl.when(has_up)
            def _():
                dn_copy(p, z, e).wait_recv()
                fs[e] += NP[p][z, e].astype(F32)

            if j:
                DP[p][r, e] = fs[e].astype(BF16)
                start(12 - p, j, DP[p].at[r, e], fin.at[q])

    def place(p):
        cols, fs, fin = ((slice(0, H2), FG, RG), (slice(H2, 3 * H), FD, RD))[p]
        dw_out[q, :, cols] = fs[q]
        for j in range(1, E):
            got(12 - p, j, fin.at[peer(j)])
            dw_out[peer(j), :, cols] = fin[peer(j)].astype(F32)

    def input_rows(s, carry):
        tot = jnp.zeros((E * T, S), F32)
        for e in range(E):
            tot = tot + lax.dot_general(
                GU[:, e * H2 : (e + 1) * H2],
                WG[s, e],
                (((1,), (1,)), ((), ())),
                preferred_element_type=F32,
            )
        DX[:, s] = tot.astype(BF16).reshape(E, T, S)
        for j in range(1, E):
            copy_to(10, j, DX.at[peer(j), s], dx_out.at[:, span(s, q)]).start()
        pltpu.make_async_copy(DX.at[q, s], dx_out.at[:, span(s, q)], loc.at[4]).start()
        return carry

    spread(1)
    for i in range(Z):
        grads(1, i)
        if i:
            chain_ends(1, i - 1)
        if i == min(1, Z - 1):
            gate_up()
    if Z > 2:
        chain(1, 1)
    spread(0)
    for i in range(Z):
        grads(0, i)
        if i:
            chain_ends(0, i - 1)
    for n in range(2, Z - 1):
        chain(1, n)
        if n < Z - 2:
            chain(0, n - 1)
    if Z > 2:
        chain(0, max(1, Z - 3))
    lax.fori_loop(0, R, input_rows, 0)
    for j in range(1, E):
        sent.append(copy_to(10, j, DX.at[q], DX.at[q]))
    for n in range(max(1, Z - 3) + 1, Z - 1):
        chain(0, n)
    finish(1)
    finish(0)
    place(1)
    place(0)
    for j in range(1, E):
        got(10, j, DX.at[peer(j)])
    pltpu.make_async_copy(DX.at[q], DX.at[q], loc.at[4]).wait()

    for d in sent:
        d.wait_send()
    for p in range(2):
        for t in range(Z):
            sib_copy(p, t).wait_send()

            def left(e, carry):
                w_copy(p, 2, t, e).wait_send()

                @pl.when((t <= z) & has_up)
                def _():
                    w_copy(p, 0, t, e).wait_send()

                @pl.when((t >= z) & has_dn)
                def _():
                    w_copy(p, 1, t, e).wait_send()

                @pl.when(t > z)
                def _():
                    up_copy(p, t, e).wait_send()

                @pl.when(t < z)
                def _():
                    dn_copy(p, t, e).wait_send()

                return carry

            lax.fori_loop(0, E, left, 0)


def by_width(tokens, grad_out, gates, expert_ids, w_all, touched):
    E, R = lax.axis_size("exp"), lax.axis_size("rep")
    T, D = tokens.shape
    S = D // (R * E)
    H = w_all.shape[2] // 3
    Z = R // 2
    w = w_all[0].reshape(E, S, 3 * H)
    ids = jnp.pad(expert_ids.astype(BF16), ((0, 0), (0, 128 - 2)))
    tm = jnp.broadcast_to(
        touched[0, 0].reshape(R, E).T.astype(F32)[:, :, None], (E, R, 128)
    )
    vm = pl.BlockSpec(memory_space=pltpu.VMEM)
    hbm = pl.BlockSpec(memory_space=pltpu.HBM)
    dma = pltpu.SemaphoreType.DMA

    def two(*lead, kind=BF16, times=1):
        return [pltpu.VMEM(lead + (times * 2 * H,), kind), pltpu.VMEM(lead + (times * H,), kind)]

    wide = pltpu.VMEM((E, R, T, S), BF16)
    tall = pltpu.VMEM((R, S, E * T), BF16)
    dx, dw = pl.pallas_call(
        functools.partial(kernel, R, E, T, S, H),
        out_shape=(
            jax.ShapeDtypeStruct((T, D), BF16),
            jax.ShapeDtypeStruct((E, S, 3 * H), F32),
        ),
        in_specs=[hbm] * 3 + [vm] * 3,
        out_specs=(hbm, vm),
        scratch_shapes=[wide, wide, tall, tall, pltpu.VMEM((E, T, 128), BF16), pltpu.VMEM((E, R, 128), F32)]
        + two(R, E, S)
        + two(E * T, kind=F32, times=E)
        + two(E, T, times=2)
        + two(E, T, times=2)
        + two(E, T, times=2)
        + two(E * T, times=E)
        + [wide]
        + two(R, E, S)
        + two(Z, E, S)
        + two(Z, E, S)
        + two(Z, E, S)
        + two(E, S, kind=F32)
        + two(E, S)
        + [
            dma((13, E)),
            dma((13, E)),
            dma((2, R, E)),
            dma((2, 3, Z, E)),
            dma((2, Z)),
            dma((2, Z)),
            dma((2, 2, Z, E)),
            dma((2, 2, Z, E)),
            dma((5,)),
        ],
        compiler_params=pltpu.CompilerParams(
            collective_id=0, has_side_effects=True, vmem_limit_bytes=52 * 1024 * 1024
        ),
    )(tokens, grad_out, w, ids, tm, gates)
    return dx, dw.reshape(1, E * S, 3 * H)


def by_expert(tokens, grad_out, gates, expert_ids, w_all, touched):
    tok_count = tokens.shape[0]
    model_width = tokens.shape[1]
    expert_count = lax.axis_size("exp")
    capacity = 5 * tok_count // (2 * expert_count)
    slot_count = expert_count * capacity
    hidden_count = w_all.shape[2] // 3
    flat_ids = expert_ids.reshape(-1)
    onehot = (flat_ids[:, None] == jnp.arange(expert_count, dtype=jnp.int32)[None, :]).astype(
        jnp.int32
    )
    slot_rank = jnp.sum(jnp.cumsum(onehot, 0) * onehot, 1) - 1
    target = flat_ids * capacity + slot_rank
    placed = target[None, :] == jnp.arange(slot_count, dtype=jnp.int32)[:, None]
    place_pair = placed.astype(jnp.bfloat16)
    place_token = jnp.sum(placed.reshape(slot_count, tok_count, 2).astype(jnp.int32), 2).astype(
        jnp.bfloat16
    )
    scaled = (grad_out.astype(jnp.float32)[:, None, :] * gates[:, :, None]).astype(jnp.bfloat16)
    scaled = scaled.reshape(2 * tok_count, model_width)
    send_x = jnp.dot(place_token, tokens, preferred_element_type=jnp.float32).astype(jnp.bfloat16)
    send_dy = jnp.dot(place_pair, scaled, preferred_element_type=jnp.float32).astype(jnp.bfloat16)
    recv_x, recv_dy = (
        lax.all_to_all(
            send_x.reshape(expert_count, capacity, model_width),
            "exp",
            split_axis=0,
            concat_axis=0,
            tiled=True,
        ),
        lax.all_to_all(
            send_dy.reshape(expert_count, capacity, model_width),
            "exp",
            split_axis=0,
            concat_axis=0,
            tiled=True,
        ),
    )
    slot_x = recv_x.reshape(slot_count, model_width)
    slot_dy = recv_dy.reshape(slot_count, model_width)
    w_local = w_all[0]
    shard_rows = lax.all_gather(w_local, "rep", axis=0, tiled=True)
    gate_up = jnp.dot(slot_x, shard_rows[:, : 2 * hidden_count], preferred_element_type=jnp.float32)
    hid_grad = jnp.dot(
        slot_dy, shard_rows[:, 2 * hidden_count :], preferred_element_type=jnp.float32
    )
    gate_pre = gate_up[:, :hidden_count]
    up_pre = gate_up[:, hidden_count:]
    silu_val, silu_slope = silu_terms(gate_pre)
    hidden = (silu_val * up_pre).astype(jnp.bfloat16)
    gate_grad = (hid_grad * up_pre * silu_slope).astype(jnp.bfloat16)
    up_grad = (hid_grad * silu_val).astype(jnp.bfloat16)
    both_grad = jnp.concatenate([gate_grad, up_grad], 1)
    row_mask = jnp.repeat(touched[0, 0].astype(jnp.float32), 128)[:, None]
    full_grad = jnp.concatenate(
        [contract_rows(slot_x, both_grad), contract_rows(slot_dy, hidden)], 1
    )
    masked = lax.optimization_barrier((full_grad * row_mask).astype(jnp.bfloat16)).astype(
        jnp.float32
    )
    owned = lax.psum_scatter(
        masked.astype(jnp.bfloat16), "rep", scatter_dimension=0, tiled=True
    ).astype(jnp.float32)
    slot_grad = lax.dot_general(
        both_grad,
        shard_rows[:, : 2 * hidden_count],
        (((1,), (1,)), ((), ())),
        preferred_element_type=jnp.float32,
    )
    slot_grad = slot_grad.astype(jnp.bfloat16)
    returned = lax.all_to_all(
        slot_grad.reshape(expert_count, capacity, model_width),
        "exp",
        split_axis=0,
        concat_axis=0,
        tiled=True,
    )
    returned = returned.reshape(slot_count, model_width)
    token_grad = contract_rows(place_token, returned).astype(jnp.bfloat16)
    return (token_grad, owned[None])


def per_device(tokens, grad_out, gates, expert_ids, w_all, touched):
    R, E = lax.axis_size("rep"), lax.axis_size("exp")
    share, rest = divmod(tokens.shape[1], R * E)
    fits = rest == 0 and share == 128 and R % 16 in (0, 8)
    fits = fits and tokens.shape[0] % 16 == 0 and w_all.shape[2] == 3 * 128
    plan = by_width if fits else by_expert
    return plan(tokens, grad_out, gates, expert_ids, w_all, touched)


def solution(mesh):
    in_specs = (
        P(("rep", "exp"), None),
        P(("rep", "exp"), None),
        P(("rep", "exp"), None),
        P(("rep", "exp"), None),
        P("exp", "rep", None),
        P("rep", "exp", None),
    )
    out_specs = (P(("rep", "exp"), None), P("exp", "rep", None))
    return jax.shard_map(
        per_device, mesh=mesh, in_specs=in_specs, out_specs=out_specs, check_vma=False
    )
```

```python
import functools
import jax
import jax.numpy as jnp
from jax import lax
from jax.experimental import pallas as pl
from jax.experimental.pallas import tpu as pltpu
from jax.sharding import PartitionSpec as P

MESH = pl.DeviceIdType.MESH
BF16 = jnp.bfloat16
F32 = jnp.float32


def silu_terms(gate_pre):
    sigmoid_g = jax.nn.sigmoid(gate_pre)
    return (gate_pre * sigmoid_g, sigmoid_g * (1.0 + gate_pre * (1.0 - sigmoid_g)))


def contract_rows(left, right):
    return lax.dot_general(
        left, right, (((0,), (0,)), ((), ())), preferred_element_type=jnp.float32
    )


def kernel(
    R, E, T, S, H,
    x_ref, g_ref, w_ref, id_ref, touch_ref, gate_ref,
    dx_out, dw_out,
    X, Y, IDS, TM, IDV, GTV, GATE, WG, WD, CG, CD, PG, PD, QG, QD, AG, AD, GU, HD, DX,
    DG, DD, BG, BD, UG, UD, NG, ND, FG, FD, RG, RD,
    a2s, a2r, wr, ws, bs, br, us, ur, loc,
):
    H2 = 2 * H
    Z = R // 2
    r = lax.axis_index("rep")
    q = lax.axis_index("exp")
    z, c = r // 2, lax.rem(r, 2)
    sib = (2 * z + 1 - c, q)
    above = (lax.rem(r + 2, R), q)
    below = (lax.rem(r + R - 2, R), q)
    has_up, has_dn = z < Z - 1, z > 0

    def peer(j):
        return lax.rem(q + j, E)

    def span(s, p):
        return pl.ds(pl.multiple_of((s * E + p) * S, S), S)

    def own_cols(s, carry):
        pltpu.make_async_copy(x_ref.at[:, span(s, q)], X.at[q, s], loc.at[0]).start()
        pltpu.make_async_copy(g_ref.at[:, span(s, q)], Y.at[q, s], loc.at[1]).start()
        return carry

    pltpu.make_async_copy(w_ref.at[q, :, :H2], WG.at[r, q], loc.at[2]).start()
    pltpu.make_async_copy(w_ref.at[q, :, H2:], WD.at[r, q], loc.at[3]).start()
    small = (
        pltpu.make_async_copy(id_ref, IDV, loc.at[5]),
        pltpu.make_async_copy(gate_ref, GTV, loc.at[6]),
        pltpu.make_async_copy(touch_ref, TM.at[q], loc.at[7]),
    )
    for d in small:
        d.start()
    lax.fori_loop(0, R, own_cols, 0)

    barrier = pltpu.get_barrier_semaphore()
    for j in range(1, E):
        pl.semaphore_signal(barrier, inc=1, device_id=(r, peer(j)), device_id_type=MESH)
    pl.semaphore_signal(barrier, inc=1, device_id=sib, device_id_type=MESH)

    @pl.when(has_up)
    def _():
        pl.semaphore_signal(barrier, inc=1, device_id=above, device_id_type=MESH)

    @pl.when(has_dn)
    def _():
        pl.semaphore_signal(barrier, inc=1, device_id=below, device_id_type=MESH)

    edge = jnp.where(z == 0, 1, 0) + jnp.where(z == Z - 1, 1, 0)
    pl.semaphore_wait(barrier, E + 2 - edge)

    def rcopy(src, dst, ss, rs, dev):
        return pltpu.make_async_remote_copy(
            src_ref=src, dst_ref=dst, send_sem=ss, recv_sem=rs, device_id=dev, device_id_type=MESH
        )

    sent = []

    def copy_to(kind, j, src, dst):
        return rcopy(src, dst, a2s.at[kind, j], a2r.at[kind, q], (r, peer(j)))

    def start(kind, j, src, dst):
        d = copy_to(kind, j, src, dst)
        d.start()
        sent.append(d)

    def got(kind, j, dst):
        p = peer(j)
        rcopy(dst, dst, a2s.at[kind, j], a2r.at[kind, p], (r, p)).wait_recv()

    WP = (WG, WD)

    def w_copy(p, way, zz, e):
        s = 2 * zz + c
        dev = (above, below, sib)[way]
        ref = WP[p].at[s, e]
        return rcopy(ref, ref, ws.at[p, way, zz, e], wr.at[p, s, e], dev)

    def w_wait(p, s, e):
        ref = WP[p].at[s, e]
        rcopy(ref, ref, ws.at[p, 2, 0, e], wr.at[p, s, e], sib).wait_recv()

    def w_slot(p, s):
        for j in range(E):
            w_wait(p, s, peer(j))

    def w_send(p, e):
        @pl.when(has_up)
        def _():
            w_copy(p, 0, z, e).start()

        @pl.when(has_dn)
        def _():
            w_copy(p, 1, z, e).start()

        w_copy(p, 2, z, e).start()

    def w_own(p):
        w_send(p, q)

    def w_first(p):
        for j in range(1, E):
            got(p, j, WP[p].at[r, peer(j)])
            w_send(p, peer(j))

    def w_forward(p, d):
        lo, hi = z - d, z + d

        def body(j, carry):
            e = lax.rem(q + j, E)

            @pl.when(lo >= 0)
            def _():
                w_wait(p, 2 * lo + c, e)

                @pl.when(has_up)
                def _():
                    w_copy(p, 0, lo, e).start()

                w_copy(p, 2, lo, e).start()

            @pl.when(hi < Z)
            def _():
                w_wait(p, 2 * hi + c, e)

                @pl.when(has_dn)
                def _():
                    w_copy(p, 1, hi, e).start()

                w_copy(p, 2, hi, e).start()

            return carry

        lax.fori_loop(0, E, body, 0)

    for j in range(1, E):
        start(0, j, w_ref.at[peer(j), :, :H2], WG.at[r, q])
    own_w = (
        pltpu.make_async_copy(w_ref.at[q, :, :H2], WG.at[r, q], loc.at[2]),
        pltpu.make_async_copy(w_ref.at[q, :, H2:], WD.at[r, q], loc.at[3]),
    )
    own_w[0].wait()
    w_own(0)
    for j in range(1, E):
        start(1, j, w_ref.at[peer(j), :, H2:], WD.at[r, q])
    own_w[1].wait()
    w_own(1)
    for d in small:
        d.wait()

    def columns(ref):
        first = lax.broadcasted_iota(jnp.int32, (T, T), 0) == 0
        return jnp.where(first, ref[0:1].astype(F32), ref[1:2].astype(F32)).T

    IDS[q] = columns(IDV).astype(BF16)
    GATE[...] = columns(GTV)
    for j in range(1, E):
        start(2, j, IDS.at[q], IDS.at[q])
        start(3, j, TM.at[q], TM.at[q])

    def send_cols(kind, src, buf):
        def body(s, carry):
            for j in range(1, E):
                copy_to(kind, j, src.at[:, span(s, peer(j))], buf.at[q, s]).start()
            return carry

        lax.fori_loop(0, R, body, 0)
        for j in range(1, E):
            sent.append(copy_to(kind, j, buf.at[q], buf.at[q]))

    send_cols(4, x_ref, X)
    send_cols(5, g_ref, Y)

    def project(p, s, first=False):
        src, wid, acc = ((X, H2, CG), (Y, H, CD))[p]
        rows = src[:, s].reshape(E * T, S)
        for e in range(E):
            v = jnp.dot(rows, WP[p][s, e], preferred_element_type=F32)
            if first:
                acc[:, e * wid : (e + 1) * wid] = v
            else:
                acc[:, e * wid : (e + 1) * wid] += v

    def project_at(p, d):
        if d == 0:
            project(p, r, True)
            w_slot(p, 2 * z + 1 - c)
            project(p, 2 * z + 1 - c)
            return
        for zz, there in ((z - d, z - d >= 0), (z + d, z + d < Z)):

            @pl.when(there)
            def _():
                project(p, 2 * zz + c)
                w_slot(p, 2 * zz + 1 - c)
                project(p, 2 * zz + 1 - c)

    w_first(0)
    w_first(1)
    for j in range(1, E):
        got(2, j, IDS.at[peer(j)])
        got(3, j, TM.at[peer(j)])
    if Z > 1:
        w_forward(0, 1)
        w_forward(1, 1)
    pltpu.make_async_copy(X.at[q], X.at[q], loc.at[0]).wait()
    for j in range(1, E):
        got(4, j, X.at[peer(j)])
    project_at(0, 0)
    for d in range(2, Z):
        w_forward(0, d)
        project_at(0, d - 1)
        if d < Z - 1:
            w_forward(1, d)
    if Z > 1:
        project_at(0, Z - 1)

    def pairs(p):
        wid, acc, buf, dst = ((H2, CG, PG, QG), (H, CD, PD, QD))[p]
        for j in list(range(1, E)) + [0]:
            o = peer(j)
            ids = IDS[o].astype(F32)
            rows = pl.ds(pl.multiple_of(o * T, T), T)
            for k in range(2):
                tot = jnp.zeros((T, wid), F32)
                for e in range(E):
                    m = (ids[:, k : k + 1] == e).astype(F32)
                    tot = tot + m * acc[rows, e * wid : (e + 1) * wid]
                buf[o, :, k * wid : (k + 1) * wid] = tot.astype(BF16)
            if j:
                start(6 + p, j, buf.at[o], dst.at[q])

    def pair_sum(p, k):
        wid, buf, dst = ((H2, PG, QG), (H, PD, QD))[p]
        tot = buf[q, :, k * wid : (k + 1) * wid].astype(F32)
        for j in range(1, E):
            tot = tot + dst[peer(j), :, k * wid : (k + 1) * wid].astype(F32)
        return tot

    pairs(0)
    pltpu.make_async_copy(Y.at[q], Y.at[q], loc.at[1]).wait()
    for j in range(1, E):
        got(5, j, Y.at[peer(j)])
    for d in range(Z - 1):
        project_at(1, d)
    if Z > 2:
        w_forward(1, Z - 1)
    project_at(1, Z - 1)
    pairs(1)
    for j in range(1, E):
        got(6, j, QG.at[peer(j)])
    acts = []
    for k in range(2):
        tot = pair_sum(0, k)
        silu_val, silu_slope = silu_terms(tot[:, :H])
        up_pre, gate = tot[:, H:], GATE[:, k : k + 1]
        acts.append((gate * up_pre * silu_slope, gate * silu_val))
        AD[q, :, k * H : (k + 1) * H] = (gate * (silu_val * up_pre)).astype(BF16)
    for j in range(1, E):
        start(8, j, AD.at[q], AD.at[q])
    for j in range(1, E):
        got(7, j, QD.at[peer(j)])
    for k in range(2):
        hid_grad = pair_sum(1, k)
        AG[q, :, k * H2 : k * H2 + H] = (hid_grad * acts[k][0]).astype(BF16)
        AG[q, :, k * H2 + H : (k + 1) * H2] = (hid_grad * acts[k][1]).astype(BF16)
    for j in range(1, E):
        start(9, j, AG.at[q], AG.at[q])

    def spread(p):
        wid, src, dst = ((H2, AG, GU), (H, AD, HD))[p]
        for j in range(E):
            o = peer(j)
            if j:
                got(9 - p, j, src.at[o])
            ids = IDS[o].astype(F32)
            rows = pl.ds(pl.multiple_of(o * T, T), T)
            a0 = src[o, :, :wid].astype(F32)
            a1 = src[o, :, wid:].astype(F32)
            for e in range(E):
                m0 = (ids[:, 0:1] == e).astype(F32)
                m1 = (ids[:, 1:2] == e).astype(F32)
                dst[rows, e * wid : (e + 1) * wid] = (m0 * a0 + m1 * a1).astype(BF16)

    DP, BP, UP, NP = (DG, DD), (BG, BD), (UG, UD), (NG, ND)

    def weight_rows(p, s):
        src, wid, act = ((X, H2, GU), (Y, H, HD))[p]
        v = contract_rows(src[:, s].reshape(E * T, S), act[...])
        for e in range(E):
            row = TM[e]
            here = lax.broadcasted_iota(jnp.int32, row.shape, 1) == s * E + q
            m = jnp.sum(jnp.where(here, row, 0), axis=1, keepdims=True).astype(F32)
            for h in range(0, wid, H):
                DP[p][s, e, :, h : h + H] = (v[:, e * wid + h : e * wid + h + H] * m).astype(BF16)

    def sib_copy(p, t):
        return rcopy(DP[p].at[2 * t + 1 - c], BP[p].at[t], bs.at[p, t], br.at[p, t], sib)

    def up_copy(p, t, e):
        src = DP[p].at[2 * t + c, e]
        return rcopy(src, UP[p].at[t, e], us.at[p, 0, t, e], ur.at[p, 0, t, e], above)

    def dn_copy(p, t, e):
        src = DP[p].at[2 * t + c, e]
        return rcopy(src, NP[p].at[t, e], us.at[p, 1, t, e], ur.at[p, 1, t, e], below)

    def grads(p, i):
        t = jnp.where(z < (Z + 1) // 2, Z - 1 - i, i)
        weight_rows(p, 2 * t + 1 - c)
        sib_copy(p, t).start()
        weight_rows(p, 2 * t + c)

    def add_in(p, t, e, others):
        tot = DP[p][2 * t + c, e].astype(F32)
        for o in others:
            tot = tot + o[t, e].astype(F32)
        DP[p][2 * t + c, e] = tot.astype(BF16)

    def chain_ends(p, n):
        def send(t, copy):
            sib_copy(p, t).wait_recv()

            def body(j, carry):
                e = lax.rem(q + j, E)
                add_in(p, t, e, (BP[p],))
                copy(p, t, e).start()
                return carry

            lax.fori_loop(1, E + 1, body, 0)

        @pl.when(z == 0)
        def _():
            send(Z - 1 - n, up_copy)

        @pl.when(z == Z - 1)
        def _():
            send(n, dn_copy)

    def chain(p, n):
        def send(t, copy, got_ref):
            sib_copy(p, t).wait_recv()

            def body(j, carry):
                e = lax.rem(q + j, E)
                copy(p, t, e).wait_recv()
                add_in(p, t, e, (BP[p], got_ref))
                copy(p, t, e).start()
                return carry

            lax.fori_loop(1, E + 1, body, 0)

        @pl.when((n >= z) & has_dn)
        def _():
            send(Z - 1 + z - n, up_copy, UP[p])

        @pl.when((n >= Z - 1 - z) & has_up)
        def _():
            send(n - (Z - 1 - z), dn_copy, NP[p])

    def finish(p):
        fs, fin = ((FG, RG), (FD, RD))[p]
        sib_copy(p, z).wait_recv()
        for j in list(range(1, E)) + [0]:
            e = peer(j)
            fs[e] = DP[p][r, e].astype(F32) + BP[p][z, e].astype(F32)

            @pl.when(has_dn)
            def _():
                up_copy(p, z, e).wait_recv()
                fs[e] += UP[p][z, e].astype(F32)

            @pl.when(has_up)
            def _():
                dn_copy(p, z, e).wait_recv()
                fs[e] += NP[p][z, e].astype(F32)

            if j:
                DP[p][r, e] = fs[e].astype(BF16)
                start(12 - p, j, DP[p].at[r, e], fin.at[q])

    def place(p):
        cols, fs, fin = ((slice(0, H2), FG, RG), (slice(H2, 3 * H), FD, RD))[p]
        dw_out[q, :, cols] = fs[q]
        for j in range(1, E):
            got(12 - p, j, fin.at[peer(j)])
            dw_out[peer(j), :, cols] = fin[peer(j)].astype(F32)

    def input_rows(s, carry):
        tot = jnp.zeros((E * T, S), F32)
        for e in range(E):
            tot = tot + lax.dot_general(
                GU[:, e * H2 : (e + 1) * H2],
                WG[s, e],
                (((1,), (1,)), ((), ())),
                preferred_element_type=F32,
            )
        DX[:, s] = tot.astype(BF16).reshape(E, T, S)
        for j in range(1, E):
            copy_to(10, j, DX.at[peer(j), s], dx_out.at[:, span(s, q)]).start()
        pltpu.make_async_copy(DX.at[q, s], dx_out.at[:, span(s, q)], loc.at[4]).start()
        return carry

    spread(1)
    for i in range(Z):
        grads(1, i)
        if i:
            chain_ends(1, i - 1)
    spread(0)
    for i in range(Z):
        grads(0, i)
        if i:
            chain_ends(0, i - 1)
        if i == Z // 2 and Z > 2:
            chain(1, 1)
    for n in range(2, Z - 1):
        chain(1, n)
        if n < Z - 2:
            chain(0, n - 1)
    if Z > 2:
        chain(0, max(1, Z - 3))
    lax.fori_loop(0, R, input_rows, 0)
    for j in range(1, E):
        sent.append(copy_to(10, j, DX.at[q], DX.at[q]))
    for n in range(max(1, Z - 3) + 1, Z - 1):
        chain(0, n)
    finish(1)
    finish(0)
    place(1)
    place(0)
    for j in range(1, E):
        got(10, j, DX.at[peer(j)])
    pltpu.make_async_copy(DX.at[q], DX.at[q], loc.at[4]).wait()

    for d in sent:
        d.wait_send()
    for p in range(2):
        for t in range(Z):
            sib_copy(p, t).wait_send()

            def left(e, carry):
                w_copy(p, 2, t, e).wait_send()

                @pl.when((t <= z) & has_up)
                def _():
                    w_copy(p, 0, t, e).wait_send()

                @pl.when((t >= z) & has_dn)
                def _():
                    w_copy(p, 1, t, e).wait_send()

                @pl.when(t > z)
                def _():
                    up_copy(p, t, e).wait_send()

                @pl.when(t < z)
                def _():
                    dn_copy(p, t, e).wait_send()

                return carry

            lax.fori_loop(0, E, left, 0)


def hand_on(dx_ref, dw_ref, dx_out, dw_out, sems):
    n = dw_ref.shape[0]
    rows = dx_ref.shape[0] // n
    copies = []
    for i in range(n):
        part = pl.ds(i * rows, rows)
        copies.append(pltpu.make_async_copy(dx_ref.at[part], dx_out.at[part], sems.at[0, i]))
        copies.append(pltpu.make_async_copy(dw_ref.at[i], dw_out.at[i], sems.at[1, i]))
    for d in copies:
        d.start()
    for d in copies:
        d.wait()


def by_width(tokens, grad_out, gates, expert_ids, w_all, touched):
    E, R = lax.axis_size("exp"), lax.axis_size("rep")
    T, D = tokens.shape
    S = D // (R * E)
    H = w_all.shape[2] // 3
    Z = R // 2
    w = w_all[0].reshape(E, S, 3 * H)
    blocks = touched.shape[2]
    vm = pl.BlockSpec(memory_space=pltpu.VMEM)
    hbm = pl.BlockSpec(memory_space=pltpu.HBM)
    dma = pltpu.SemaphoreType.DMA

    def two(*lead, kind=BF16, times=1):
        return [pltpu.VMEM(lead + (times * 2 * H,), kind), pltpu.VMEM(lead + (times * H,), kind)]

    wide = pltpu.VMEM((E, R, T, S), BF16)
    dx, dw = pl.pallas_call(
        functools.partial(kernel, R, E, T, S, H),
        out_shape=(
            jax.ShapeDtypeStruct((T, D), BF16),
            jax.ShapeDtypeStruct((E, S, 3 * H), F32),
        ),
        in_specs=[hbm] * 6,
        out_specs=(vm, vm),
        scratch_shapes=[wide, wide, pltpu.VMEM((E, T, 128), BF16), pltpu.VMEM((E, 1, blocks), jnp.int32)]
        + [pltpu.VMEM((2, T), jnp.int32), pltpu.VMEM((2, T), F32), pltpu.VMEM((T, T), F32)]
        + two(R, E, S)
        + two(E * T, kind=F32, times=E)
        + two(E, T, times=2)
        + two(E, T, times=2)
        + two(E, T, times=2)
        + two(E * T, times=E)
        + [wide]
        + two(R, E, S)
        + two(Z, E, S)
        + two(Z, E, S)
        + two(Z, E, S)
        + two(E, S, kind=F32)
        + two(E, S)
        + [
            dma((13, E)),
            dma((13, E)),
            dma((2, R, E)),
            dma((2, 3, Z, E)),
            dma((2, Z)),
            dma((2, Z)),
            dma((2, 2, Z, E)),
            dma((2, 2, Z, E)),
            dma((8,)),
        ],
        compiler_params=pltpu.CompilerParams(
            collective_id=0, has_side_effects=True, vmem_limit_bytes=60 * 1024 * 1024
        ),
    )(tokens, grad_out, w, expert_ids.T, touched[0], gates.T)
    some = pl.BlockSpec(memory_space=pl.ANY)
    dx, dw = pl.pallas_call(
        hand_on,
        out_shape=(
            jax.ShapeDtypeStruct((T, D), BF16),
            jax.ShapeDtypeStruct((E, S, 3 * H), F32),
        ),
        in_specs=[some] * 2,
        out_specs=(hbm, hbm),
        scratch_shapes=[dma((2, E))],
        compiler_params=pltpu.CompilerParams(vmem_limit_bytes=60 * 1024 * 1024),
    )(dx, dw)
    return dx, dw.reshape(1, E * S, 3 * H)


def by_expert(tokens, grad_out, gates, expert_ids, w_all, touched):
    tok_count = tokens.shape[0]
    model_width = tokens.shape[1]
    expert_count = lax.axis_size("exp")
    capacity = 5 * tok_count // (2 * expert_count)
    slot_count = expert_count * capacity
    hidden_count = w_all.shape[2] // 3
    flat_ids = expert_ids.reshape(-1)
    onehot = (flat_ids[:, None] == jnp.arange(expert_count, dtype=jnp.int32)[None, :]).astype(
        jnp.int32
    )
    slot_rank = jnp.sum(jnp.cumsum(onehot, 0) * onehot, 1) - 1
    target = flat_ids * capacity + slot_rank
    placed = target[None, :] == jnp.arange(slot_count, dtype=jnp.int32)[:, None]
    place_pair = placed.astype(jnp.bfloat16)
    place_token = jnp.sum(placed.reshape(slot_count, tok_count, 2).astype(jnp.int32), 2).astype(
        jnp.bfloat16
    )
    scaled = (grad_out.astype(jnp.float32)[:, None, :] * gates[:, :, None]).astype(jnp.bfloat16)
    scaled = scaled.reshape(2 * tok_count, model_width)
    send_x = jnp.dot(place_token, tokens, preferred_element_type=jnp.float32).astype(jnp.bfloat16)
    send_dy = jnp.dot(place_pair, scaled, preferred_element_type=jnp.float32).astype(jnp.bfloat16)
    recv_x, recv_dy = (
        lax.all_to_all(
            send_x.reshape(expert_count, capacity, model_width),
            "exp",
            split_axis=0,
            concat_axis=0,
            tiled=True,
        ),
        lax.all_to_all(
            send_dy.reshape(expert_count, capacity, model_width),
            "exp",
            split_axis=0,
            concat_axis=0,
            tiled=True,
        ),
    )
    slot_x = recv_x.reshape(slot_count, model_width)
    slot_dy = recv_dy.reshape(slot_count, model_width)
    w_local = w_all[0]
    shard_rows = lax.all_gather(w_local, "rep", axis=0, tiled=True)
    gate_up = jnp.dot(slot_x, shard_rows[:, : 2 * hidden_count], preferred_element_type=jnp.float32)
    hid_grad = jnp.dot(
        slot_dy, shard_rows[:, 2 * hidden_count :], preferred_element_type=jnp.float32
    )
    gate_pre = gate_up[:, :hidden_count]
    up_pre = gate_up[:, hidden_count:]
    silu_val, silu_slope = silu_terms(gate_pre)
    hidden = (silu_val * up_pre).astype(jnp.bfloat16)
    gate_grad = (hid_grad * up_pre * silu_slope).astype(jnp.bfloat16)
    up_grad = (hid_grad * silu_val).astype(jnp.bfloat16)
    both_grad = jnp.concatenate([gate_grad, up_grad], 1)
    row_mask = jnp.repeat(touched[0, 0].astype(jnp.float32), 128)[:, None]
    full_grad = jnp.concatenate(
        [contract_rows(slot_x, both_grad), contract_rows(slot_dy, hidden)], 1
    )
    masked = lax.optimization_barrier((full_grad * row_mask).astype(jnp.bfloat16)).astype(
        jnp.float32
    )
    owned = lax.psum_scatter(
        masked.astype(jnp.bfloat16), "rep", scatter_dimension=0, tiled=True
    ).astype(jnp.float32)
    slot_grad = lax.dot_general(
        both_grad,
        shard_rows[:, : 2 * hidden_count],
        (((1,), (1,)), ((), ())),
        preferred_element_type=jnp.float32,
    )
    slot_grad = slot_grad.astype(jnp.bfloat16)
    returned = lax.all_to_all(
        slot_grad.reshape(expert_count, capacity, model_width),
        "exp",
        split_axis=0,
        concat_axis=0,
        tiled=True,
    )
    returned = returned.reshape(slot_count, model_width)
    token_grad = contract_rows(place_token, returned).astype(jnp.bfloat16)
    return (token_grad, owned[None])


def per_device(tokens, grad_out, gates, expert_ids, w_all, touched):
    R, E = lax.axis_size("rep"), lax.axis_size("exp")
    share, rest = divmod(tokens.shape[1], R * E)
    fits = rest == 0 and share == 128 and R % 16 in (0, 8)
    fits = fits and tokens.shape[0] == 128 and w_all.shape[2] == 3 * 128
    plan = by_width if fits else by_expert
    return plan(tokens, grad_out, gates, expert_ids, w_all, touched)


def solution(mesh):
    in_specs = (
        P(("rep", "exp"), None),
        P(("rep", "exp"), None),
        P(("rep", "exp"), None),
        P(("rep", "exp"), None),
        P("exp", "rep", None),
        P("rep", "exp", None),
    )
    out_specs = (P(("rep", "exp"), None), P("exp", "rep", None))
    return jax.shard_map(
        per_device, mesh=mesh, in_specs=in_specs, out_specs=out_specs, check_vma=False
    )
```

```python
import functools
import jax
import jax.numpy as jnp
from jax import lax
from jax.experimental import pallas as pl
from jax.experimental.pallas import tpu as pltpu
from jax.sharding import PartitionSpec as P

MESH = pl.DeviceIdType.MESH
BF16 = jnp.bfloat16
F32 = jnp.float32


def silu_terms(gate_pre):
    sigmoid_g = jax.nn.sigmoid(gate_pre)
    return (gate_pre * sigmoid_g, sigmoid_g * (1.0 + gate_pre * (1.0 - sigmoid_g)))


def contract_rows(left, right):
    return lax.dot_general(
        left, right, (((0,), (0,)), ((), ())), preferred_element_type=jnp.float32
    )


def kernel(
    R, E, T, S, H,
    x_ref, g_ref, w_ref, id_ref, touch_ref, gate_ref,
    dx_out, dw_out,
    X, Y, IDS, TM, IDV, GTV, GATE, WG, WD, CG, CD, PG, PD, QG, QD, AG, AD, GU, HD, DX,
    DG, DD, BG, BD, UG, UD, NG, ND, FG, FD, RG, RD,
    a2s, a2r, wr, ws, bs, br, us, ur, loc,
):
    H2 = 2 * H
    Z = R // 2
    r = lax.axis_index("rep")
    q = lax.axis_index("exp")
    z, c = r // 2, lax.rem(r, 2)
    sib = (2 * z + 1 - c, q)
    above = (lax.rem(r + 2, R), q)
    below = (lax.rem(r + R - 2, R), q)
    has_up, has_dn = z < Z - 1, z > 0

    def peer(j):
        return lax.rem(q + j, E)

    def span(s, p):
        return pl.ds(pl.multiple_of((s * E + p) * S, S), S)

    def own_cols(s, carry):
        pltpu.make_async_copy(x_ref.at[:, span(s, q)], X.at[q, s], loc.at[0]).start()
        pltpu.make_async_copy(g_ref.at[:, span(s, q)], Y.at[q, s], loc.at[1]).start()
        return carry

    pltpu.make_async_copy(w_ref.at[q, :, :H2], WG.at[r, q], loc.at[2]).start()
    pltpu.make_async_copy(w_ref.at[q, :, H2:], WD.at[r, q], loc.at[3]).start()
    small = (
        pltpu.make_async_copy(id_ref, IDV, loc.at[5]),
        pltpu.make_async_copy(gate_ref, GTV, loc.at[6]),
        pltpu.make_async_copy(touch_ref, TM.at[q], loc.at[7]),
    )
    for d in small:
        d.start()
    lax.fori_loop(0, R, own_cols, 0)

    barrier = pltpu.get_barrier_semaphore()
    for j in range(1, E):
        pl.semaphore_signal(barrier, inc=1, device_id=(r, peer(j)), device_id_type=MESH)
    pl.semaphore_signal(barrier, inc=1, device_id=sib, device_id_type=MESH)

    @pl.when(has_up)
    def _():
        pl.semaphore_signal(barrier, inc=1, device_id=above, device_id_type=MESH)

    @pl.when(has_dn)
    def _():
        pl.semaphore_signal(barrier, inc=1, device_id=below, device_id_type=MESH)

    edge = jnp.where(z == 0, 1, 0) + jnp.where(z == Z - 1, 1, 0)
    pl.semaphore_wait(barrier, E + 2 - edge)

    def rcopy(src, dst, ss, rs, dev):
        return pltpu.make_async_remote_copy(
            src_ref=src, dst_ref=dst, send_sem=ss, recv_sem=rs, device_id=dev, device_id_type=MESH
        )

    sent = []

    def copy_to(kind, j, src, dst):
        return rcopy(src, dst, a2s.at[kind, j], a2r.at[kind, q], (r, peer(j)))

    def start(kind, j, src, dst):
        d = copy_to(kind, j, src, dst)
        d.start()
        sent.append(d)

    def got(kind, j, dst):
        p = peer(j)
        rcopy(dst, dst, a2s.at[kind, j], a2r.at[kind, p], (r, p)).wait_recv()

    WP = (WG, WD)

    def w_copy(p, way, zz, e):
        s = 2 * zz + c
        dev = (above, below, sib)[way]
        ref = WP[p].at[s, e]
        return rcopy(ref, ref, ws.at[p, way, zz, e], wr.at[p, s, e], dev)

    def w_wait(p, s, e):
        ref = WP[p].at[s, e]
        rcopy(ref, ref, ws.at[p, 2, 0, e], wr.at[p, s, e], sib).wait_recv()

    def w_slot(p, s):
        for j in range(E):
            w_wait(p, s, peer(j))

    def w_send(p, e):
        @pl.when(has_up)
        def _():
            w_copy(p, 0, z, e).start()

        @pl.when(has_dn)
        def _():
            w_copy(p, 1, z, e).start()

        w_copy(p, 2, z, e).start()

    def w_own(p):
        w_send(p, q)

    def w_first(p):
        for j in range(1, E):
            got(p, j, WP[p].at[r, peer(j)])
            w_send(p, peer(j))

    def w_forward(p, d):
        lo, hi = z - d, z + d

        def body(j, carry):
            e = lax.rem(q + j, E)

            @pl.when(lo >= 0)
            def _():
                w_wait(p, 2 * lo + c, e)

                @pl.when(has_up)
                def _():
                    w_copy(p, 0, lo, e).start()

                w_copy(p, 2, lo, e).start()

            @pl.when(hi < Z)
            def _():
                w_wait(p, 2 * hi + c, e)

                @pl.when(has_dn)
                def _():
                    w_copy(p, 1, hi, e).start()

                w_copy(p, 2, hi, e).start()

            return carry

        lax.fori_loop(0, E, body, 0)

    for j in range(1, E):
        start(0, j, w_ref.at[peer(j), :, :H2], WG.at[r, q])
    own_w = (
        pltpu.make_async_copy(w_ref.at[q, :, :H2], WG.at[r, q], loc.at[2]),
        pltpu.make_async_copy(w_ref.at[q, :, H2:], WD.at[r, q], loc.at[3]),
    )
    own_w[0].wait()
    w_own(0)
    for j in range(1, E):
        start(1, j, w_ref.at[peer(j), :, H2:], WD.at[r, q])
    own_w[1].wait()
    w_own(1)
    for d in small:
        d.wait()

    def columns(ref):
        first = lax.broadcasted_iota(jnp.int32, (T, T), 0) == 0
        return jnp.where(first, ref[0:1].astype(F32), ref[1:2].astype(F32)).T

    IDS[q] = columns(IDV).astype(BF16)
    GATE[...] = columns(GTV)
    for j in range(1, E):
        start(2, j, IDS.at[q], IDS.at[q])
        start(3, j, TM.at[q], TM.at[q])

    def send_cols(kind, src, buf):
        def body(s, carry):
            for j in range(1, E):
                copy_to(kind, j, src.at[:, span(s, peer(j))], buf.at[q, s]).start()
            return carry

        lax.fori_loop(0, R, body, 0)
        for j in range(1, E):
            sent.append(copy_to(kind, j, buf.at[q], buf.at[q]))

    send_cols(4, x_ref, X)
    send_cols(5, g_ref, Y)

    def project(p, s, first=False):
        src, wid, acc = ((X, H2, CG), (Y, H, CD))[p]
        rows = src[:, s].reshape(E * T, S)
        for e in range(E):
            v = jnp.dot(rows, WP[p][s, e], preferred_element_type=F32)
            if first:
                acc[:, e * wid : (e + 1) * wid] = v
            else:
                acc[:, e * wid : (e + 1) * wid] += v

    def project_at(p, d):
        if d == 0:
            project(p, r, True)
            w_slot(p, 2 * z + 1 - c)
            project(p, 2 * z + 1 - c)
            return
        for zz, there in ((z - d, z - d >= 0), (z + d, z + d < Z)):

            @pl.when(there)
            def _():
                project(p, 2 * zz + c)
                w_slot(p, 2 * zz + 1 - c)
                project(p, 2 * zz + 1 - c)

    w_first(0)
    w_first(1)
    for j in range(1, E):
        got(2, j, IDS.at[peer(j)])
        got(3, j, TM.at[peer(j)])
    if Z > 1:
        w_forward(0, 1)
        w_forward(1, 1)
    pltpu.make_async_copy(X.at[q], X.at[q], loc.at[0]).wait()
    for j in range(1, E):
        got(4, j, X.at[peer(j)])
    project_at(0, 0)
    for d in range(2, Z):
        w_forward(0, d)
        project_at(0, d - 1)
        if d < Z - 1:
            w_forward(1, d)
    if Z > 1:
        project_at(0, Z - 1)

    def pairs(p):
        wid, acc, buf, dst = ((H2, CG, PG, QG), (H, CD, PD, QD))[p]
        for j in list(range(1, E)) + [0]:
            o = peer(j)
            ids = IDS[o].astype(F32)
            rows = pl.ds(pl.multiple_of(o * T, T), T)
            for k in range(2):
                tot = jnp.zeros((T, wid), F32)
                for e in range(E):
                    m = (ids[:, k : k + 1] == e).astype(F32)
                    tot = tot + m * acc[rows, e * wid : (e + 1) * wid]
                buf[o, :, k * wid : (k + 1) * wid] = tot.astype(BF16)
            if j:
                start(6 + p, j, buf.at[o], dst.at[q])

    def pair_sum(p, k):
        wid, buf, dst = ((H2, PG, QG), (H, PD, QD))[p]
        tot = buf[q, :, k * wid : (k + 1) * wid].astype(F32)
        for j in range(1, E):
            tot = tot + dst[peer(j), :, k * wid : (k + 1) * wid].astype(F32)
        return tot

    pairs(0)
    pltpu.make_async_copy(Y.at[q], Y.at[q], loc.at[1]).wait()
    for j in range(1, E):
        got(5, j, Y.at[peer(j)])
    for d in range(Z - 1):
        project_at(1, d)
    if Z > 2:
        w_forward(1, Z - 1)
    project_at(1, Z - 1)
    pairs(1)
    for j in range(1, E):
        got(6, j, QG.at[peer(j)])
    acts = []
    for k in range(2):
        tot = pair_sum(0, k)
        silu_val, silu_slope = silu_terms(tot[:, :H])
        up_pre, gate = tot[:, H:], GATE[:, k : k + 1]
        acts.append((gate * up_pre * silu_slope, gate * silu_val))
        AD[q, :, k * H : (k + 1) * H] = (gate * (silu_val * up_pre)).astype(BF16)
    for j in range(1, E):
        start(8, j, AD.at[q], AD.at[q])
    for j in range(1, E):
        got(7, j, QD.at[peer(j)])
    for k in range(2):
        hid_grad = pair_sum(1, k)
        AG[q, :, k * H2 : k * H2 + H] = (hid_grad * acts[k][0]).astype(BF16)
        AG[q, :, k * H2 + H : (k + 1) * H2] = (hid_grad * acts[k][1]).astype(BF16)
    for j in range(1, E):
        start(9, j, AG.at[q], AG.at[q])

    def spread(p):
        wid, src, dst = ((H2, AG, GU), (H, AD, HD))[p]
        for j in range(E):
            o = peer(j)
            if j:
                got(9 - p, j, src.at[o])
            ids = IDS[o].astype(F32)
            rows = pl.ds(pl.multiple_of(o * T, T), T)
            a0 = src[o, :, :wid].astype(F32)
            a1 = src[o, :, wid:].astype(F32)
            for e in range(E):
                m0 = (ids[:, 0:1] == e).astype(F32)
                m1 = (ids[:, 1:2] == e).astype(F32)
                dst[rows, e * wid : (e + 1) * wid] = (m0 * a0 + m1 * a1).astype(BF16)

    DP, BP, UP, NP = (DG, DD), (BG, BD), (UG, UD), (NG, ND)

    def weight_rows(p, s):
        src, wid, act = ((X, H2, GU), (Y, H, HD))[p]
        v = contract_rows(src[:, s].reshape(E * T, S), act[...])
        for e in range(E):
            row = TM[e]
            here = lax.broadcasted_iota(jnp.int32, row.shape, 1) == s * E + q
            m = jnp.sum(jnp.where(here, row, 0), axis=1, keepdims=True).astype(F32)
            for h in range(0, wid, H):
                DP[p][s, e, :, h : h + H] = (v[:, e * wid + h : e * wid + h + H] * m).astype(BF16)

    def sib_copy(p, t):
        return rcopy(DP[p].at[2 * t + 1 - c], BP[p].at[t], bs.at[p, t], br.at[p, t], sib)

    def up_copy(p, t, e):
        src = DP[p].at[2 * t + c, e]
        return rcopy(src, UP[p].at[t, e], us.at[p, 0, t, e], ur.at[p, 0, t, e], above)

    def dn_copy(p, t, e):
        src = DP[p].at[2 * t + c, e]
        return rcopy(src, NP[p].at[t, e], us.at[p, 1, t, e], ur.at[p, 1, t, e], below)

    def grads(p, i):
        t = jnp.where(z < (Z + 1) // 2, Z - 1 - i, i)
        weight_rows(p, 2 * t + 1 - c)
        sib_copy(p, t).start()
        weight_rows(p, 2 * t + c)

    def add_in(p, t, e, others):
        tot = DP[p][2 * t + c, e].astype(F32)
        for o in others:
            tot = tot + o[t, e].astype(F32)
        DP[p][2 * t + c, e] = tot.astype(BF16)

    def chain_ends(p, n):
        def send(t, copy):
            sib_copy(p, t).wait_recv()

            def body(j, carry):
                e = lax.rem(q + j, E)
                add_in(p, t, e, (BP[p],))
                copy(p, t, e).start()
                return carry

            lax.fori_loop(1, E + 1, body, 0)

        @pl.when(z == 0)
        def _():
            send(Z - 1 - n, up_copy)

        @pl.when(z == Z - 1)
        def _():
            send(n, dn_copy)

    def chain(p, n):
        def send(t, copy, got_ref):
            sib_copy(p, t).wait_recv()

            def body(j, carry):
                e = lax.rem(q + j, E)
                copy(p, t, e).wait_recv()
                add_in(p, t, e, (BP[p], got_ref))
                copy(p, t, e).start()
                return carry

            lax.fori_loop(1, E + 1, body, 0)

        @pl.when((n >= z) & has_dn)
        def _():
            send(Z - 1 + z - n, up_copy, UP[p])

        @pl.when((n >= Z - 1 - z) & has_up)
        def _():
            send(n - (Z - 1 - z), dn_copy, NP[p])

    def finish(p):
        fs, fin = ((FG, RG), (FD, RD))[p]
        sib_copy(p, z).wait_recv()
        for j in list(range(1, E)) + [0]:
            e = peer(j)
            fs[e] = DP[p][r, e].astype(F32) + BP[p][z, e].astype(F32)

            @pl.when(has_dn)
            def _():
                up_copy(p, z, e).wait_recv()
                fs[e] += UP[p][z, e].astype(F32)

            @pl.when(has_up)
            def _():
                dn_copy(p, z, e).wait_recv()
                fs[e] += NP[p][z, e].astype(F32)

            if j:
                DP[p][r, e] = fs[e].astype(BF16)
                start(12 - p, j, DP[p].at[r, e], fin.at[q])

    def place(p):
        cols, fs, fin = ((slice(0, H2), FG, RG), (slice(H2, 3 * H), FD, RD))[p]
        dw_out[q, :, cols] = fs[q]
        for j in range(1, E):
            got(12 - p, j, fin.at[peer(j)])
            dw_out[peer(j), :, cols] = fin[peer(j)].astype(F32)

    def input_rows(s, carry):
        tot = jnp.zeros((E * T, S), F32)
        for e in range(E):
            tot = tot + lax.dot_general(
                GU[:, e * H2 : (e + 1) * H2],
                WG[s, e],
                (((1,), (1,)), ((), ())),
                preferred_element_type=F32,
            )
        DX[:, s] = tot.astype(BF16).reshape(E, T, S)
        for j in range(1, E):
            copy_to(10, j, DX.at[peer(j), s], dx_out.at[:, span(s, q)]).start()
        pltpu.make_async_copy(DX.at[q, s], dx_out.at[:, span(s, q)], loc.at[4]).start()
        return carry

    spread(1)
    for i in range(Z):
        grads(1, i)
        if i:
            chain_ends(1, i - 1)
    spread(0)
    for i in range(Z):
        grads(0, i)
        if i:
            chain_ends(0, i - 1)
        if i == Z // 2 and Z > 2:
            chain(1, 1)
    for n in range(2, Z - 1):
        chain(1, n)
        if n < Z - 2:
            chain(0, n - 1)
    if Z > 2:
        chain(0, max(1, Z - 3))
    lax.fori_loop(0, R, input_rows, 0)
    for j in range(1, E):
        sent.append(copy_to(10, j, DX.at[q], DX.at[q]))
    for n in range(max(1, Z - 3) + 1, Z - 1):
        chain(0, n)
    finish(1)
    finish(0)
    place(1)
    place(0)
    for j in range(1, E):
        got(10, j, DX.at[peer(j)])
    pltpu.make_async_copy(DX.at[q], DX.at[q], loc.at[4]).wait()

    for d in sent:
        d.wait_send()
    for p in range(2):
        for t in range(Z):
            sib_copy(p, t).wait_send()

            def left(e, carry):
                w_copy(p, 2, t, e).wait_send()

                @pl.when((t <= z) & has_up)
                def _():
                    w_copy(p, 0, t, e).wait_send()

                @pl.when((t >= z) & has_dn)
                def _():
                    w_copy(p, 1, t, e).wait_send()

                @pl.when(t > z)
                def _():
                    up_copy(p, t, e).wait_send()

                @pl.when(t < z)
                def _():
                    dn_copy(p, t, e).wait_send()

                return carry

            lax.fori_loop(0, E, left, 0)


def hand_on(dx_ref, dw_ref, dx_out, dw_out):
    dx_out[...] = dx_ref[...]
    dw_out[...] = dw_ref[...]


def by_width(tokens, grad_out, gates, expert_ids, w_all, touched):
    E, R = lax.axis_size("exp"), lax.axis_size("rep")
    T, D = tokens.shape
    S = D // (R * E)
    H = w_all.shape[2] // 3
    Z = R // 2
    w = w_all[0].reshape(E, S, 3 * H)
    blocks = touched.shape[2]
    vm = pl.BlockSpec(memory_space=pltpu.VMEM)
    hbm = pl.BlockSpec(memory_space=pltpu.HBM)
    dma = pltpu.SemaphoreType.DMA

    def two(*lead, kind=BF16, times=1):
        return [pltpu.VMEM(lead + (times * 2 * H,), kind), pltpu.VMEM(lead + (times * H,), kind)]

    wide = pltpu.VMEM((E, R, T, S), BF16)
    dx, dw = pl.pallas_call(
        functools.partial(kernel, R, E, T, S, H),
        out_shape=(
            jax.ShapeDtypeStruct((T, D), BF16),
            jax.ShapeDtypeStruct((E, S, 3 * H), F32),
        ),
        in_specs=[hbm] * 6,
        out_specs=(vm, vm),
        scratch_shapes=[wide, wide, pltpu.VMEM((E, T, 128), BF16), pltpu.VMEM((E, 1, blocks), jnp.int32)]
        + [pltpu.VMEM((2, T), jnp.int32), pltpu.VMEM((2, T), F32), pltpu.VMEM((T, T), F32)]
        + two(R, E, S)
        + two(E * T, kind=F32, times=E)
        + two(E, T, times=2)
        + two(E, T, times=2)
        + two(E, T, times=2)
        + two(E * T, times=E)
        + [wide]
        + two(R, E, S)
        + two(Z, E, S)
        + two(Z, E, S)
        + two(Z, E, S)
        + two(E, S, kind=F32)
        + two(E, S)
        + [
            dma((13, E)),
            dma((13, E)),
            dma((2, R, E)),
            dma((2, 3, Z, E)),
            dma((2, Z)),
            dma((2, Z)),
            dma((2, 2, Z, E)),
            dma((2, 2, Z, E)),
            dma((8,)),
        ],
        compiler_params=pltpu.CompilerParams(
            collective_id=0, has_side_effects=True, vmem_limit_bytes=60 * 1024 * 1024
        ),
    )(tokens, grad_out, w, expert_ids.T, touched[0], gates.T)
    parts = [
        pl.BlockSpec((T // E, D), lambda i: (i, 0)),
        pl.BlockSpec((1, S, 3 * H), lambda i: (i, 0, 0)),
    ]
    dx, dw = pl.pallas_call(
        hand_on,
        grid=(E,),
        out_shape=(
            jax.ShapeDtypeStruct((T, D), BF16),
            jax.ShapeDtypeStruct((E, S, 3 * H), F32),
        ),
        in_specs=parts,
        out_specs=parts,
        compiler_params=pltpu.CompilerParams(vmem_limit_bytes=60 * 1024 * 1024),
    )(dx, dw)
    return dx, dw.reshape(1, E * S, 3 * H)


def by_expert(tokens, grad_out, gates, expert_ids, w_all, touched):
    tok_count = tokens.shape[0]
    model_width = tokens.shape[1]
    expert_count = lax.axis_size("exp")
    capacity = 5 * tok_count // (2 * expert_count)
    slot_count = expert_count * capacity
    hidden_count = w_all.shape[2] // 3
    flat_ids = expert_ids.reshape(-1)
    onehot = (flat_ids[:, None] == jnp.arange(expert_count, dtype=jnp.int32)[None, :]).astype(
        jnp.int32
    )
    slot_rank = jnp.sum(jnp.cumsum(onehot, 0) * onehot, 1) - 1
    target = flat_ids * capacity + slot_rank
    placed = target[None, :] == jnp.arange(slot_count, dtype=jnp.int32)[:, None]
    place_pair = placed.astype(jnp.bfloat16)
    place_token = jnp.sum(placed.reshape(slot_count, tok_count, 2).astype(jnp.int32), 2).astype(
        jnp.bfloat16
    )
    scaled = (grad_out.astype(jnp.float32)[:, None, :] * gates[:, :, None]).astype(jnp.bfloat16)
    scaled = scaled.reshape(2 * tok_count, model_width)
    send_x = jnp.dot(place_token, tokens, preferred_element_type=jnp.float32).astype(jnp.bfloat16)
    send_dy = jnp.dot(place_pair, scaled, preferred_element_type=jnp.float32).astype(jnp.bfloat16)
    recv_x, recv_dy = (
        lax.all_to_all(
            send_x.reshape(expert_count, capacity, model_width),
            "exp",
            split_axis=0,
            concat_axis=0,
            tiled=True,
        ),
        lax.all_to_all(
            send_dy.reshape(expert_count, capacity, model_width),
            "exp",
            split_axis=0,
            concat_axis=0,
            tiled=True,
        ),
    )
    slot_x = recv_x.reshape(slot_count, model_width)
    slot_dy = recv_dy.reshape(slot_count, model_width)
    w_local = w_all[0]
    shard_rows = lax.all_gather(w_local, "rep", axis=0, tiled=True)
    gate_up = jnp.dot(slot_x, shard_rows[:, : 2 * hidden_count], preferred_element_type=jnp.float32)
    hid_grad = jnp.dot(
        slot_dy, shard_rows[:, 2 * hidden_count :], preferred_element_type=jnp.float32
    )
    gate_pre = gate_up[:, :hidden_count]
    up_pre = gate_up[:, hidden_count:]
    silu_val, silu_slope = silu_terms(gate_pre)
    hidden = (silu_val * up_pre).astype(jnp.bfloat16)
    gate_grad = (hid_grad * up_pre * silu_slope).astype(jnp.bfloat16)
    up_grad = (hid_grad * silu_val).astype(jnp.bfloat16)
    both_grad = jnp.concatenate([gate_grad, up_grad], 1)
    row_mask = jnp.repeat(touched[0, 0].astype(jnp.float32), 128)[:, None]
    full_grad = jnp.concatenate(
        [contract_rows(slot_x, both_grad), contract_rows(slot_dy, hidden)], 1
    )
    masked = lax.optimization_barrier((full_grad * row_mask).astype(jnp.bfloat16)).astype(
        jnp.float32
    )
    owned = lax.psum_scatter(
        masked.astype(jnp.bfloat16), "rep", scatter_dimension=0, tiled=True
    ).astype(jnp.float32)
    slot_grad = lax.dot_general(
        both_grad,
        shard_rows[:, : 2 * hidden_count],
        (((1,), (1,)), ((), ())),
        preferred_element_type=jnp.float32,
    )
    slot_grad = slot_grad.astype(jnp.bfloat16)
    returned = lax.all_to_all(
        slot_grad.reshape(expert_count, capacity, model_width),
        "exp",
        split_axis=0,
        concat_axis=0,
        tiled=True,
    )
    returned = returned.reshape(slot_count, model_width)
    token_grad = contract_rows(place_token, returned).astype(jnp.bfloat16)
    return (token_grad, owned[None])


def per_device(tokens, grad_out, gates, expert_ids, w_all, touched):
    R, E = lax.axis_size("rep"), lax.axis_size("exp")
    share, rest = divmod(tokens.shape[1], R * E)
    fits = rest == 0 and share == 128 and tokens.shape[0] % (16 * E) == 0
    fits = fits and tokens.shape[0] == 128 and w_all.shape[2] == 3 * 128
    plan = by_width if fits else by_expert
    return plan(tokens, grad_out, gates, expert_ids, w_all, touched)


def solution(mesh):
    in_specs = (
        P(("rep", "exp"), None),
        P(("rep", "exp"), None),
        P(("rep", "exp"), None),
        P(("rep", "exp"), None),
        P("exp", "rep", None),
        P("rep", "exp", None),
    )
    out_specs = (P(("rep", "exp"), None), P("exp", "rep", None))
    return jax.shard_map(
        per_device, mesh=mesh, in_specs=in_specs, out_specs=out_specs, check_vma=False
    )
```
